32 devices in a mesh: grp: 2 (over y), pool: 4 (over z), head: 2 (over x), aux: 2 (over core).
Axes of the slice: x: 2, y: 2, z: 4, core: 2. Of those that a mesh axis runs over, the one named last changes fastest.
Arguments:
- hidden: bfloat16 [16, 8192], P('grp', ('pool', 'head', 'aux')), parts along dimension 0, may hold values from -0.59765625 to 0.59765625
- gain: float32 [8192], P(('pool', 'head', 'aux')), may hold values from 0.5 to 1.5
- queries: bfloat16 [16, 8192], P(('grp', 'pool'), 'aux'), parts along dimension 0, may hold values from -6 to 6
- new_key: bfloat16 [16, 1024], P(('grp', 'pool'), 'aux'), parts along dimension 0, may hold values from -6 to 6
- new_value: bfloat16 [16, 1024], P(('grp', 'pool'), 'aux'), parts along dimension 0, may hold values from -6 to 6
- cache_key: bfloat16 [16, 512, 1024], P(('grp', 'pool'), 'head', 'aux'), parts along dimension 0, may hold values from -6 to 6
- cache_value: bfloat16 [16, 512, 1024], P(('grp', 'pool'), 'head', 'aux'), parts along dimension 0, may hold values from -6 to 6
- lengths: int32 [16], P('grp'), parts along dimension 0, may hold values from 170 to 512, as said below
- slot_of: int32 [16], P('grp'), parts along dimension 0, may hold values from 0 to 7, as said below
- out_proj: bfloat16 [2, 4096, 8192], P('aux', 'head', 'pool'), may hold values from -0.09375 to 0.09375
- lm_head: bfloat16 [8192, 65536], P(None, ('pool', 'head', 'aux')), may hold values from -1 to 1
Outputs:
- logits: float32 [16, 65536], P('grp', ('pool', 'head', 'aux')), parts along dimension 0
- entropy: float32 [16], P('grp'), parts along dimension 0
The draws below stay inside these ranges and needn't reach their ends.
There are 2 independent parts, one for each index of `grp`. The reference program is written for one: setup_inputs(seed, part) draws one part's arguments, and reference() takes and returns one part's arrays. A program takes and returns all parts, laid end to end along the dimension named above; an argument that names none is the same for every part. Nothing has to cross between parts.
Inputs may be any that keep to these rules, and one draw needn't show every extreme that they name: `lengths`: some request fills all 512 positions and some has exactly 170. `slot_of`: each slot holds exactly one request; the requests of one index of pool have their slots together on one index of pool.
All inputs are finite; a program needn't handle non-finite values.
Results may differ from the reference program's by a relative error of at most 0.02.
Values may be sent and summed in bfloat16 or wider, within the bound.
A program may use at most 128 MiB of HBM per device.

```python
import math
import jax
import jax.numpy as jnp
from jax import lax

D = 8192
QH = 64
KVH = 8
HD = 128
VOCAB = 65536
REQ_DEV = 2
CAP = 512
REQS = 8
N_POOL = 4
N_AUX = 2


def draw_lengths(key, part):
    lowest = CAP // 3
    base = jax.random.randint(jax.random.fold_in(key, 11), (REQS,), lowest, CAP + 1)
    first = jax.random.randint(jax.random.fold_in(key, 12), (), 0, REQS)
    offset = jax.random.randint(jax.random.fold_in(key, 13), (), 1, REQS)
    second = (first + offset) % REQS
    places = jnp.arange(REQS, dtype=jnp.int32)
    base = jnp.where(places == first, CAP, base)
    base = jnp.where(places == second, lowest, base)
    return base.astype(jnp.int32)


def draw_slot_of(key, part):
    count = N_POOL
    if count >= 4:
        cycle = [0, 1, 1 + count // 2, count // 2]
    elif count >= 2:
        cycle = [0, 1]
    else:
        cycle = [0]
    targets = cycle[1:] + cycle[:1]
    others = [place for place in range(count) if place not in cycle]
    mapping = jnp.zeros((count,), jnp.int32)
    mapping = mapping.at[jnp.array(cycle, dtype=jnp.int32)].set(jnp.array(targets, dtype=jnp.int32))
    if len(others) > 0:
        rest = jnp.array(others, dtype=jnp.int32)
        mixing = jax.random.permutation(jax.random.fold_in(key, 31), len(others))
        mapping = mapping.at[rest].set(rest[mixing])
    rotate = jax.random.randint(jax.random.fold_in(key, 32), (), 0, count)
    inner = jax.random.randint(jax.random.fold_in(key, 33), (count,), 0, REQ_DEV)
    request = jnp.arange(REQS, dtype=jnp.int32)
    home = request // REQ_DEV
    target = (mapping[(home - rotate) % count] + rotate) % count
    within = (request % REQ_DEV + inner[home]) % REQ_DEV
    return (target * REQ_DEV + within).astype(jnp.int32)


def draw_lm_head(key, part):
    column = jnp.arange(VOCAB, dtype=jnp.float32) / (VOCAB - 1)
    rise = 1.0 + column
    jitter = jnp.exp(jax.random.uniform(jax.random.fold_in(key, 21), (VOCAB,), minval=0.0, maxval=math.log(2.0)))
    entries = jax.random.truncated_normal(jax.random.fold_in(key, 22), -4.0, 4.0, (D, VOCAB))
    scaled = entries * (rise * jitter)[None, :] / math.sqrt(D)
    scaled = jnp.clip(scaled, -1.0, 1.0)
    return scaled.astype(jnp.bfloat16)


def with_spikes(drawn, rng, source, target, blocks, factor):
    def block_of(axis_at):
        return (jnp.arange(drawn.shape[axis_at]) // (drawn.shape[axis_at] // blocks)).reshape((-1,) + (1,) * (drawn.ndim - 1 - axis_at))

    first = jax.random.permutation(rng, blocks)[block_of(target)]
    other_side = (block_of(target) + blocks // 2) % blocks
    return jnp.where((block_of(source) == first) | (block_of(source) == other_side), factor * drawn, drawn)


def block_levels(own_key, dims, pieces, low, top_value):
    def one(dim, parts):
        steps = jax.random.uniform(jax.random.fold_in(jax.random.fold_in(own_key, 6), dim), (parts,), jnp.float32, low / len(pieces), top_value / len(pieces))
        return jnp.repeat(jnp.exp(steps), dims[dim] // parts).reshape((-1,) + (1,) * (len(dims) - dim - 1))

    level = one(*pieces[0])
    for cut in pieces[1:]:
        level = level * one(*cut)
    return level


def bell_draw(own_key, shape, deviation, bound, pieces=(), kind=jnp.bfloat16):
    drawn = jax.random.normal(own_key, shape, jnp.float32) * deviation
    if len(pieces) > 0:
        drawn = block_levels(own_key, shape, pieces, -0.22, 0.18) * drawn
    return jnp.clip(drawn, min=-bound, max=bound).astype(kind)


def heavy_noise(key, dims, scale, reach, cuts, heavy, held_as=jnp.bfloat16):
    result = scale * jax.random.normal(key, dims, jnp.float32)
    if cuts:
        result = result * block_levels(key, dims, cuts, -0.22, 0.18)
    return jnp.clip(with_spikes(result, jax.random.fold_in(key, 3), *heavy), -reach, reach).astype(held_as)


def setup_inputs(seed: int = 0, part: int = 0) -> dict:
    splits = jax.random.split(jax.random.key(seed), 12)
    part_splits = jax.random.split(jax.random.fold_in(splits[11], part), 12)
    hidden = bell_draw(part_splits[0], (REQS, D), 0.1, 0.59765625, ((1, 16),))
    gain = jnp.clip(1.0 + 0.1 * jax.random.normal(splits[1], (D,), jnp.float32), 0.5, 1.5)
    queries = bell_draw(part_splits[2], (REQS, QH * HD), 1.0, 6.0, ((0, 4), (1, 2)))
    new_key = bell_draw(part_splits[3], (REQS, KVH * HD), 1.0, 6.0, ((0, 4), (1, 2)))
    new_value = bell_draw(part_splits[4], (REQS, KVH * HD), 1.0, 6.0, ((0, 4), (1, 2)))
    cache_key = bell_draw(part_splits[5], (REQS, CAP, KVH * HD), 1.0, 6.0, ((0, 4), (1, 2), (2, 2)))
    cache_value = bell_draw(part_splits[6], (REQS, CAP, KVH * HD), 1.0, 6.0, ((0, 4), (1, 2), (2, 2)))
    lengths = draw_lengths(jax.random.fold_in(jax.random.fold_in(splits[11], part), 71), part)
    slot_of = draw_slot_of(jax.random.fold_in(jax.random.fold_in(splits[11], part), 71), part)
    out_proj = heavy_noise(splits[9], (N_AUX, QH * HD // N_AUX, D), (QH * HD) ** -0.5, 0.09375, ((0, 2), (1, 2), (2, 4)), (1, 2, 4, 2.0))
    lm_head = draw_lm_head(jax.random.fold_in(splits[11], 71), part)
    return dict(hidden=hidden, gain=gain, queries=queries, new_key=new_key, new_value=new_value, cache_key=cache_key, cache_value=cache_value, lengths=lengths, slot_of=slot_of, out_proj=out_proj, lm_head=lm_head)


def reference(hidden, gain, queries, new_key, new_value, cache_key, cache_value, lengths, slot_of, out_proj, lm_head):
    group = QH // KVH
    scale = 1.0 / math.sqrt(HD)
    keys = jnp.take(cache_key, slot_of, axis=0).reshape(REQS, CAP, KVH, HD).astype(jnp.float32)
    values = jnp.take(cache_value, slot_of, axis=0).reshape(REQS, CAP, KVH, HD).astype(jnp.float32)
    query_heads = queries.reshape(REQS, KVH, group, HD).astype(jnp.float32)
    scores = jnp.einsum('rkgd,rtkd->rkgt', query_heads, keys, precision=lax.Precision.HIGHEST) * scale
    position = jnp.arange(CAP, dtype=jnp.int32)
    live = position[None, :] < lengths[:, None]
    weights = jnp.where(live[:, None, None, :], jnp.exp(scores), 0.0)
    rounded = lax.optimization_barrier(weights.astype(jnp.bfloat16)).astype(jnp.float32)
    own_keys = new_key.reshape(REQS, KVH, 1, HD).astype(jnp.float32)
    own_values = new_value.reshape(REQS, KVH, 1, HD).astype(jnp.float32)
    own = jnp.exp(lax.optimization_barrier(jnp.sum(query_heads * own_keys, axis=3)) * scale)
    total = lax.optimization_barrier(jnp.sum(weights, axis=3)) + own
    mixed = jnp.einsum('rkgt,rtkd->rkgd', rounded, values, precision=lax.Precision.HIGHEST)
    mixed = mixed + own[..., None] * own_values
    attended = (mixed / total[..., None]).astype(jnp.bfloat16).reshape(REQS, QH * HD)
    projected = jnp.dot(attended, out_proj.reshape(QH * HD, D), preferred_element_type=jnp.float32)
    stream = (hidden.astype(jnp.float32) + projected).astype(jnp.bfloat16)
    stream = lax.optimization_barrier(stream).astype(jnp.float32)
    mean_sq = lax.optimization_barrier(jnp.mean(stream * stream, axis=1, keepdims=True))
    normed = (stream * lax.rsqrt(mean_sq + 1e-05) * gain[None, :]).astype(jnp.bfloat16)
    logits = jnp.dot(normed, lm_head, preferred_element_type=jnp.float32)
    expd = jnp.exp(logits)
    vocab_total = lax.optimization_barrier(jnp.sum(expd, axis=1))
    moment = lax.optimization_barrier(jnp.sum(expd * logits, axis=1))
    entropy = jnp.log(vocab_total) - moment / vocab_total
    return (logits, entropy)
```

```python
import functools
import math

import jax
import jax.numpy as jnp
from jax import lax
from jax.experimental import pallas as pl
from jax.experimental.pallas import tpu as pltpu
from jax.sharding import PartitionSpec as P

HD = 128
MESH = pl.DeviceIdType.MESH
BF = jnp.bfloat16
F32 = jnp.float32
MIB = 1024 * 1024
RING = 15


def iota(shape, axis):
    return lax.broadcasted_iota(jnp.int32, shape, axis)


def mm(a, b):
    return jnp.dot(a, b, preferred_element_type=F32)


def pick(position, scalars):
    out = jnp.full(position.shape, scalars[0], jnp.int32)
    for r in range(1, len(scalars)):
        out = jnp.where(position == r, scalars[r], out)
    return out


def kernel(
    cfg,
    slot_ref,
    len_ref,
    hidden_hbm,
    gain_hbm,
    q_hbm,
    nk_hbm,
    nv_hbm,
    ck_hbm,
    cv_hbm,
    wo_hbm,
    lm_hbm,
    logits_hbm,
    ent_ref,
    ring,
    ck,
    cv,
    qv,
    nkv,
    nvv,
    hid,
    gains,
    stage,
    xq,
    send2,
    recv2,
    send3,
    recv3,
    xs,
    acc,
    xe,
    ring_sem,
    wo_sem,
    in_sem,
    out_sem,
    q_send,
    q_recv,
    g_send,
    g_recv,
    a_send,
    a_recv,
    t_send,
    t_recv,
    s_send,
    s_recv,
    e_send,
    e_recv,
):
    NP, NH, NA = cfg["NP"], cfg["NH"], cfg["NA"]
    R, S, KV, G, SPAN = cfg["R"], cfg["S"], cfg["KV"], cfg["G"], cfg["SPAN"]
    W, NCH, NBUF = cfg["W"], cfg["NCH"], cfg["NBUF"]
    QL = KV * G
    HO = QL // NH
    QUAD = NH * NA
    scale = 1.0 / math.sqrt(HD)
    p = lax.axis_index("pool")
    h = lax.axis_index("head")
    a = lax.axis_index("aux")
    me = (p * NH + h) * NA + a
    everyone = [
        (dp, dh, da)
        for dp in range(NP)
        for dh in range(NH)
        for da in range(NA)
        if (dp, dh, da) != (0, 0, 0)
    ]

    def at(dp, dh, da):
        return {
            "pool": lax.rem(p + dp, NP),
            "head": lax.rem(h + dh, NH),
            "aux": lax.rem(a + da, NA),
        }

    def place(where):
        return (where["pool"] * NH + where["head"]) * NA + where["aux"]

    barrier = pltpu.get_barrier_semaphore()
    for d in everyone:
        pl.semaphore_signal(barrier, inc=1, device_id=at(*d), device_id_type=MESH)

    ins = [
        pltpu.make_async_copy(src, dst, in_sem.at[i])
        for i, (src, dst) in enumerate(
            [
                (q_hbm, qv),
                (nk_hbm, nkv),
                (nv_hbm, nvv),
                (gain_hbm, gains.at[me]),
                (hidden_hbm, hid),
                (ck_hbm, ck),
                (cv_hbm, cv),
            ]
        )
    ]
    for c in ins:
        c.start()

    DB = wo_hbm.shape[2]
    ROWS, VL = ring.shape[1], ring.shape[2]
    per = VL // DB
    KO = wo_hbm.shape[1]
    pieces = KO // ROWS
    held_slots = pieces // per
    wo_places = [
        (NBUF - held_slots + i // per, (i % per) * DB, i * ROWS) for i in range(pieces)
    ]
    wo_copies = [
        pltpu.make_async_copy(
            wo_hbm.at[0, pl.ds(row, ROWS), :],
            ring.at[slot, :, pl.ds(lane, DB)],
            wo_sem.at[i],
        )
        for i, (slot, lane, row) in enumerate(wo_places)
    ]
    for c in wo_copies:
        c.start()

    def block_of(o):
        return lax.rem(p * QUAD + o, NCH)

    def lm_copy(o, slot):
        row = pl.multiple_of(block_of(o) * ROWS, ROWS)
        return pltpu.make_async_copy(
            lm_hbm.at[pl.ds(row, ROWS), :], ring.at[slot], ring_sem.at[slot]
        )

    for o in range(NBUF - held_slots):
        lm_copy(o, o).start()

    for c in ins[:4]:
        c.wait()
    for j in range(QL):
        stage[j * S : (j + 1) * S, :] = qv[:, j * HD : (j + 1) * HD].astype(F32)
    for j in range(KV):
        stage[(QL + j) * S : (QL + j + 1) * S, :] = nkv[:, j * HD : (j + 1) * HD].astype(F32)
        stage[(QL + KV + j) * S : (QL + KV + j + 1) * S, :] = nvv[
            :, j * HD : (j + 1) * HD
        ].astype(F32)
    xq[p] = stage[...].astype(BF)

    pl.semaphore_wait(barrier, len(everyone))

    def send(src, dst, ssem, rsem, to):
        c = pltpu.make_async_remote_copy(
            src_ref=src, dst_ref=dst, send_sem=ssem, recv_sem=rsem,
            device_id=to, device_id_type=MESH,
        )
        c.start()
        return c

    sent = []
    q_copies = [
        send(xq.at[p], xq.at[p], q_send.at[d], q_recv.at[d], at(d, 0, 0))
        for d in range(1, NP)
    ]
    sent += q_copies
    for i, d in enumerate(everyone):
        sent.append(send(gains.at[me], gains.at[me], g_send.at[i], g_recv.at[me], at(*d)))

    slots = [slot_ref[r] for r in range(R)]
    lengths = [len_ref[r] for r in range(R)]
    rows_q = iota((S * QL, NP * QL * S), 0)
    cols_q = iota((S * QL, NP * QL * S), 1)
    req_q = (cols_q // (QL * S)) * S + cols_q % S
    hot_q = jnp.where(
        ((cols_q // S) % QL == rows_q % QL) & (pick(req_q, slots) == p * S + rows_q // QL),
        1.0,
        0.0,
    ).astype(BF)
    M2 = 2 * KV * S
    rows_k = iota((2 * S * QL, NP * M2), 0)
    cols_k = iota((2 * S * QL, NP * M2), 1)
    req_k = (cols_k // M2) * S + cols_k % S
    hot_k = jnp.where(
        ((cols_k // S) % (2 * KV) == (rows_k // (S * QL)) * KV + (rows_k % QL) // G)
        & (pick(req_k, slots) == p * S + (rows_k % (S * QL)) // QL),
        1.0,
        0.0,
    ).astype(BF)
    position = h * SPAN + iota((G, SPAN), 1)
    live = []
    for s in range(S):
        length = jnp.int32(0)
        for r in range(R):
            length = length + jnp.where(slots[r] == p * S + s, lengths[r], 0)
        live.append(position < length)

    for c in q_copies:
        c.wait_recv()
    Xq = xq[:, 0 : QL * S, :].reshape(NP * QL * S, HD)
    Xk = xq[:, QL * S :, :].reshape(NP * M2, HD)
    Qs = mm(hot_q, Xq)
    KVs = mm(hot_k, Xk)
    own = jnp.exp(jnp.sum(Qs * KVs[: S * QL], axis=1, keepdims=True) * scale)
    own = own * jnp.where(h == 0, 1.0, 0.0)

    for c in ins[5:]:
        c.wait()
    total_parts, mixed_parts = [], []
    for s in range(S):
        for k in range(KV):
            at_row = (s * KV + k) * G
            query = Qs[at_row : at_row + G].astype(BF)
            scores = lax.dot_general(
                query,
                ck[s, :, k * HD : (k + 1) * HD],
                (((1,), (1,)), ((), ())),
                preferred_element_type=F32,
            )
            weights = jnp.where(live[s], jnp.exp(scores * scale), 0.0)
            total_parts.append(jnp.sum(weights, axis=1, keepdims=True))
            mixed_parts.append(mm(weights.astype(BF), cv[s, :, k * HD : (k + 1) * HD]))
    total = jnp.concatenate(total_parts, axis=0) + own
    mixed = jnp.concatenate(mixed_parts, axis=0) + own * KVs[S * QL :]
    B = S * HO
    diag = iota((B, HD), 0) == iota((B, HD), 1)
    lines = iota((16, HD), 0)
    for t in range(NH):
        column = []
        for s in range(S):
            first = s * QL + t * HO
            send2[t, s * HO : (s + 1) * HO, :] = mixed[first : first + HO].astype(BF)
            column.append(total[first : first + HO])
        column = jnp.concatenate(column, axis=0)
        line = jnp.sum(jnp.where(diag, column, 0.0), axis=0, keepdims=True)
        high = line.astype(BF).astype(F32)
        send2[t, B:, :] = jnp.where(
            lines == 0, high, jnp.where(lines == 1, line - high, 0.0)
        ).astype(BF)
    here = p * NH + h
    recv2[here] = send2[h]
    a_copies = []
    for i, (dp, dh, da) in enumerate([d for d in everyone if d[2] == 0]):
        to = at(dp, dh, 0)
        a_copies.append(
            send(send2.at[to["head"]], recv2.at[here], a_send.at[i], a_recv.at[i], to)
        )
    sent += a_copies

    RH = iota((HO * R, NP * B), 0)
    CH = iota((HO * R, NP * B), 1)
    order = jnp.where(
        (RH // R == CH % HO) & (pick(RH % R, slots) == CH // HO), 1.0, 0.0
    ).astype(BF)
    for c in a_copies:
        c.wait_recv()
    attended = []
    for q in range(NP):
        got = recv2[q * NH].astype(F32)
        for t in range(1, NH):
            got = got + recv2[q * NH + t].astype(F32)
        line = got[B : B + 1] + got[B + 1 : B + 2]
        column = jnp.sum(jnp.where(diag, line, 0.0), axis=1, keepdims=True)
        attended.append((got[:B] / column).astype(BF))
    by_head = mm(order, jnp.concatenate(attended, axis=0))
    by_request = jnp.concatenate(
        [by_head[j * R : (j + 1) * R] for j in range(HO)], axis=1
    ).astype(BF)

    for c in wo_copies:
        c.wait()
    mine = h * NA + a
    for n in range(QUAD):
        term = jnp.zeros((R, W), F32)
        for slot, lane, row in wo_places:
            term = term + mm(
                by_request[:, row : row + ROWS], ring[slot, :, lane + n * W : lane + (n + 1) * W]
            )
        send3[n] = term
    recv3[mine] = send3[mine]
    t_copies = []
    for i, (dp, dh, da) in enumerate([d for d in everyone if d[0] == 0]):
        to = at(0, dh, da)
        t_copies.append(
            send(
                send3.at[to["head"] * NA + to["aux"]],
                recv3.at[mine],
                t_send.at[i],
                t_recv.at[i],
                to,
            )
        )
    sent += t_copies
    for o in range(NBUF - held_slots, NBUF):
        lm_copy(o, o).start()
    ins[4].wait()
    for c in t_copies:
        c.wait_recv()
    stream = hid[...].astype(F32)
    projected = recv3[0]
    for n in range(1, QUAD):
        projected = projected + recv3[n]
    stream = stream + projected
    xs[me] = jnp.concatenate([stream[:, : W // 2], stream[:, W // 2 :]], axis=0).astype(BF)
    for i, d in enumerate(everyone):
        sent.append(send(xs.at[me], xs.at[me], s_send.at[i], s_recv.at[me], at(*d)))

    acc[...] = jnp.zeros_like(acc)

    def step(o, squares):
        b = block_of(o)
        slot = lax.rem(o, NBUF)

        @pl.when(b != me)
        def _():
            pltpu.make_async_remote_copy(
                src_ref=gains.at[b], dst_ref=gains.at[b], send_sem=g_send.at[0],
                recv_sem=g_recv.at[b], device_id=at(1, 0, 0), device_id_type=MESH,
            ).wait_recv()
            pltpu.make_async_remote_copy(
                src_ref=xs.at[b], dst_ref=xs.at[b], send_sem=s_send.at[0],
                recv_sem=s_recv.at[b], device_id=at(1, 0, 0), device_id_type=MESH,
            ).wait_recv()

        halves = xs[b].astype(F32)
        block = jnp.concatenate([halves[:R], halves[R:]], axis=1)
        left = (block * gains[b]).astype(BF)
        lm_copy(o, slot).wait()
        acc[...] += mm(left, ring[slot])

        @pl.when(o + NBUF < NCH)
        def _():
            lm_copy(o + NBUF, slot).start()

        return squares + jnp.sum(block * block, axis=1, keepdims=True)

    squares = lax.fori_loop(0, NCH, step, jnp.zeros((R, 1), F32))
    logits = acc[...] * lax.rsqrt(squares * (1.0 / (NCH * ROWS)) + 1e-05)
    acc[...] = logits
    out = pltpu.make_async_copy(acc, logits_hbm, out_sem)
    out.start()
    expd = jnp.exp(logits)
    sums = jnp.sum(expd, axis=1, keepdims=True)
    moments = jnp.sum(expd * logits, axis=1, keepdims=True)
    lane = iota((R, HD), 1)
    xe[me] = jnp.where(lane == 0, sums, jnp.where(lane == 1, moments, 0.0))
    e_copies = [
        send(xe.at[me], xe.at[me], e_send.at[i], e_recv.at[i], at(*d))
        for i, d in enumerate(everyone)
    ]
    sent += e_copies
    for c in e_copies:
        c.wait_recv()
    both = jnp.sum(xe[...], axis=0)
    vocab_total, moment = both[:, 0:1], both[:, 1:2]
    entropy = jnp.log(vocab_total) - moment / vocab_total
    spread = jnp.sum(jnp.where(iota((R, HD), 0) == lane, entropy, 0.0), axis=0, keepdims=True)
    ent_ref[...] = spread[:, :R]
    out.wait()
    for c in sent:
        c.wait_send()


def one_kernel(
    cfg,
    hidden, gain, queries, new_key, new_value, cache_key, cache_value, lengths, slot_of,
    out_proj, lm_head,
):
    NP, NH, NA = cfg["NP"], cfg["NH"], cfg["NA"]
    R, S, KV, G, SPAN = cfg["R"], cfg["S"], cfg["KV"], cfg["G"], cfg["SPAN"]
    W, NCH, NBUF = cfg["W"], cfg["NCH"], cfg["NBUF"]
    QL = KV * G
    N = NP * NH * NA
    QUAD = NH * NA
    VL = lm_head.shape[1]
    rows = (QL + 2 * KV) * S
    message = S * (QL // NH) + 16
    DMA = pltpu.SemaphoreType.DMA
    smem = pl.BlockSpec(memory_space=pltpu.SMEM)
    anywhere = pl.BlockSpec(memory_space=pl.ANY)
    weights = lm_head.size + out_proj.size + 2 * cache_key.size
    logits, entropy = pl.pallas_call(
        functools.partial(kernel, cfg),
        out_shape=(
            jax.ShapeDtypeStruct((R, VL), F32),
            jax.ShapeDtypeStruct((1, R), F32),
        ),
        in_specs=[smem, smem] + [anywhere] * 9,
        out_specs=(anywhere, pl.BlockSpec(memory_space=pltpu.VMEM)),
        scratch_shapes=[
            pltpu.VMEM((NBUF, W, VL), BF),
            pltpu.VMEM(cache_key.shape, BF),
            pltpu.VMEM(cache_value.shape, BF),
            pltpu.VMEM(queries.shape, BF),
            pltpu.VMEM(new_key.shape, BF),
            pltpu.VMEM(new_value.shape, BF),
            pltpu.VMEM(hidden.shape, BF),
            pltpu.VMEM((N, 1, W), F32),
            pltpu.VMEM((rows, HD), F32),
            pltpu.VMEM((NP, rows, HD), BF),
            pltpu.VMEM((NH, message, HD), BF),
            pltpu.VMEM((NP * NH, message, HD), BF),
            pltpu.VMEM((QUAD, R, W), F32),
            pltpu.VMEM((QUAD, R, W), F32),
            pltpu.VMEM((N, 2 * R, W // 2), BF),
            pltpu.VMEM((R, VL), F32),
            pltpu.VMEM((N, R, HD), F32),
            DMA((NBUF,)),
            DMA((out_proj.shape[1] // W,)),
            DMA((7,)),
            DMA,
            DMA((NP,)),
            DMA((NP,)),
            DMA((N,)),
            DMA((N,)),
            DMA((NP * NH,)),
            DMA((NP * NH,)),
            DMA((QUAD,)),
            DMA((QUAD,)),
            DMA((N,)),
            DMA((N,)),
            DMA((N,)),
            DMA((N,)),
        ],
        compiler_params=pltpu.CompilerParams(
            collective_id=0, has_side_effects=True, vmem_limit_bytes=63 * MIB
        ),
        cost_estimate=pl.CostEstimate(
            flops=2 * R * weights, bytes_accessed=2 * weights, transcendentals=R * VL
        ),
    )(
        slot_of, lengths, hidden, gain.reshape(1, W), queries, new_key, new_value,
        cache_key, cache_value, out_proj, lm_head,
    )
    return logits, entropy.reshape(R)


def arrangement(mesh, args):
    NP, NH, NA = mesh.shape["pool"], mesh.shape["head"], mesh.shape["aux"]
    hidden, queries, cache_key, out_proj, lm_head = (
        args[0], args[2], args[5], args[9], args[10],
    )
    R, W = hidden.shape
    S, SPAN = cache_key.shape[:2]
    KV = cache_key.shape[2] // HD
    QL = queries.shape[1] // HD
    VL = lm_head.shape[1]
    HO = out_proj.shape[1] // HD
    fits = (
        R == 8
        and W % 256 == 0
        and VL % out_proj.shape[2] == 0
        and out_proj.shape[1] % W == 0
        and (out_proj.shape[1] // W) % (VL // out_proj.shape[2]) == 0
        and HO % 16 == 0
        and S * HO <= HD
        and QL // KV == 8
        and (KV * S) % 8 == 0
        and SPAN % 128 == 0
        and W * VL * 2 * RING <= 60 * MIB
    )
    if not fits:
        return None
    return dict(
        NP=NP, NH=NH, NA=NA, R=R, S=S, KV=KV, G=QL // KV, SPAN=SPAN, W=W,
        NCH=lm_head.shape[0] // W, NBUF=min(RING, lm_head.shape[0] // W),
    )


def select_rows(onehot, rows):
    return jnp.dot(onehot.astype(jnp.bfloat16), rows, preferred_element_type=jnp.float32).astype(
        jnp.bfloat16
    )


def per_device(
    hidden,
    gain,
    queries,
    new_key,
    new_value,
    cache_key,
    cache_value,
    lengths,
    slot_of,
    out_proj,
    lm_head,
):
    slots_here = cache_key.shape[0]
    span = cache_key.shape[1]
    kv_here = cache_key.shape[2] // HD
    q_here = queries.shape[1] // HD
    group = q_here // kv_here
    heads_out = out_proj.shape[1] // HD
    scale = 1.0 / math.sqrt(HD)
    pool_place = lax.axis_index("pool")
    head_place = lax.axis_index("head")
    all_queries, all_keys, all_values = (
        lax.all_gather(queries, "pool", axis=0, tiled=True),
        lax.all_gather(new_key, "pool", axis=0, tiled=True),
        lax.all_gather(new_value, "pool", axis=0, tiled=True),
    )
    requests = all_queries.shape[0]
    slot_ids = pool_place * slots_here + jnp.arange(slots_here, dtype=jnp.int32)
    chosen = slot_of[None, :] == slot_ids[:, None]
    query_slot = select_rows(chosen, all_queries)
    key_slot = select_rows(chosen, all_keys)
    value_slot = select_rows(chosen, all_values)
    length_slot = jnp.sum(jnp.where(chosen, lengths[None, :], 0), axis=1)
    query_heads = query_slot.reshape(slots_here, kv_here, group, HD)
    keys = cache_key.reshape(slots_here, span, kv_here, HD)
    values = cache_value.reshape(slots_here, span, kv_here, HD)
    scores = (
        jnp.einsum("skgd,stkd->skgt", query_heads, keys, preferred_element_type=jnp.float32) * scale
    )
    position = head_place * span + jnp.arange(span, dtype=jnp.int32)
    live = position[None, :] < length_slot[:, None]
    weights = jnp.where(live[:, None, None, :], jnp.exp(scores), 0.0)
    total = jnp.sum(weights, axis=3).reshape(slots_here, q_here)
    mixed = jnp.einsum(
        "skgt,stkd->skgd", weights.astype(jnp.bfloat16), values, preferred_element_type=jnp.float32
    )
    mixed = mixed.reshape(slots_here, q_here * HD)
    total, mixed = (
        lax.psum(total.astype(jnp.bfloat16), "head").astype(jnp.float32),
        lax.psum(mixed.astype(jnp.bfloat16), "head").astype(jnp.float32),
    )
    total = lax.dynamic_slice_in_dim(total, head_place * heads_out, heads_out, 1)
    mixed = lax.dynamic_slice_in_dim(mixed, head_place * heads_out * HD, heads_out * HD, 1)
    query_own = lax.dynamic_slice_in_dim(query_slot, head_place * heads_out * HD, heads_out * HD, 1)
    query_own = query_own.reshape(slots_here, heads_out, HD).astype(jnp.float32)
    key_spread = jnp.repeat(key_slot.reshape(slots_here, kv_here, HD), group, axis=1)
    value_spread = jnp.repeat(value_slot.reshape(slots_here, kv_here, HD), group, axis=1)
    key_own = lax.dynamic_slice_in_dim(key_spread, head_place * heads_out, heads_out, 1).astype(
        jnp.float32
    )
    value_own = lax.dynamic_slice_in_dim(value_spread, head_place * heads_out, heads_out, 1).astype(
        jnp.float32
    )
    own = jnp.exp(jnp.sum(query_own * key_own, axis=2) * scale)
    total = total + own
    mixed = mixed.reshape(slots_here, heads_out, HD) + own[:, :, None] * value_own
    attended = (mixed / total[:, :, None]).astype(jnp.bfloat16).reshape(slots_here, heads_out * HD)
    outputs = lax.all_gather(attended, "pool", axis=0, tiled=True)
    order = slot_of[:, None] == jnp.arange(requests, dtype=jnp.int32)[None, :]
    by_request = select_rows(order, outputs)
    weight_block = out_proj[0]
    term = jnp.dot(by_request, weight_block, preferred_element_type=jnp.float32)
    projected = lax.psum(term.astype(jnp.bfloat16), ("head", "aux")).astype(jnp.float32)
    block_hidden, block_gain = (
        lax.all_gather(hidden, ("head", "aux"), axis=1, tiled=True),
        lax.all_gather(gain.astype(jnp.bfloat16), ("head", "aux"), axis=0, tiled=True).astype(
            gain.dtype
        ),
    )
    stream = (block_hidden.astype(jnp.float32) + projected).astype(jnp.bfloat16)
    full_stream, full_gain = (
        lax.all_gather(stream, "pool", axis=1, tiled=True),
        lax.all_gather(block_gain.astype(jnp.bfloat16), "pool", axis=0, tiled=True).astype(
            block_gain.dtype
        ),
    )
    stream_wide = full_stream.astype(jnp.float32)
    mean_sq = jnp.mean(stream_wide * stream_wide, axis=1, keepdims=True)
    normed = (stream_wide * lax.rsqrt(mean_sq + 1e-05) * full_gain[None, :]).astype(jnp.bfloat16)
    logits = jnp.dot(normed, lm_head, preferred_element_type=jnp.float32)
    expd = jnp.exp(logits)
    vocab_total, moment = lax.psum(
        (jnp.sum(expd, axis=1), jnp.sum(expd * logits, axis=1)), ("pool", "head", "aux")
    )
    entropy = jnp.log(vocab_total) - moment / vocab_total
    return (logits, entropy)


def solution(mesh):
    in_specs = (
        P("grp", ("pool", "head", "aux")),
        P(("pool", "head", "aux")),
        P(("grp", "pool"), "aux"),
        P(("grp", "pool"), "aux"),
        P(("grp", "pool"), "aux"),
        P(("grp", "pool"), "head", "aux"),
        P(("grp", "pool"), "head", "aux"),
        P("grp"),
        P("grp"),
        P("aux", "head", "pool"),
        P(None, ("pool", "head", "aux")),
    )
    out_specs = (P("grp", ("pool", "head", "aux")), P("grp"))

    def on_device(*args):
        cfg = arrangement(mesh, args)
        if cfg is None:
            return per_device(*args)
        return one_kernel(cfg, *args)

    return jax.shard_map(
        on_device, mesh=mesh, in_specs=in_specs, out_specs=out_specs, check_vma=False
    )
```

```python
import functools
import math

import jax
import jax.numpy as jnp
from jax import lax
from jax.experimental import pallas as pl
from jax.experimental.pallas import tpu as pltpu
from jax.sharding import PartitionSpec as P

HD = 128
MESH = pl.DeviceIdType.MESH
BF = jnp.bfloat16
F32 = jnp.float32
MIB = 1024 * 1024
RING = 15


def iota(shape, axis):
    return lax.broadcasted_iota(jnp.int32, shape, axis)


def mm(a, b):
    return jnp.dot(a, b, preferred_element_type=F32)


def pick(position, scalars):
    out = jnp.full(position.shape, scalars[0], jnp.int32)
    for r in range(1, len(scalars)):
        out = jnp.where(position == r, scalars[r], out)
    return out


def kernel(
    cfg,
    slot_ref,
    len_ref,
    hidden_hbm,
    gain_hbm,
    q_hbm,
    nk_hbm,
    nv_hbm,
    ck_hbm,
    cv_hbm,
    wo_hbm,
    lm_hbm,
    logits_hbm,
    ent_ref,
    ring,
    ck,
    cv,
    qv,
    nkv,
    nvv,
    hid,
    gains,
    stage,
    xq,
    send2,
    recv2,
    send3,
    recv3,
    xs,
    acc,
    xe,
    ring_sem,
    wo_sem,
    in_sem,
    out_sem,
    q_send,
    q_recv,
    g_send,
    g_recv,
    a_send,
    a_recv,
    t_send,
    t_recv,
    s_send,
    s_recv,
    e_send,
    e_recv,
):
    NP, NH, NA = cfg["NP"], cfg["NH"], cfg["NA"]
    R, S, KV, G, SPAN = cfg["R"], cfg["S"], cfg["KV"], cfg["G"], cfg["SPAN"]
    W, NCH, NBUF = cfg["W"], cfg["NCH"], cfg["NBUF"]
    QL = KV * G
    HO = QL // NH
    QUAD = NH * NA
    scale = 1.0 / math.sqrt(HD)
    p = lax.axis_index("pool")
    h = lax.axis_index("head")
    a = lax.axis_index("aux")
    me = (p * NH + h) * NA + a
    everyone = [
        (dp, dh, da)
        for dp in range(NP)
        for dh in range(NH)
        for da in range(NA)
        if (dp, dh, da) != (0, 0, 0)
    ]

    def at(dp, dh, da):
        return {
            "pool": lax.rem(p + dp, NP),
            "head": lax.rem(h + dh, NH),
            "aux": lax.rem(a + da, NA),
        }

    def place(where):
        return (where["pool"] * NH + where["head"]) * NA + where["aux"]

    barrier = pltpu.get_barrier_semaphore()
    for d in everyone:
        pl.semaphore_signal(barrier, inc=1, device_id=at(*d), device_id_type=MESH)

    ins = [
        pltpu.make_async_copy(src, dst, in_sem.at[i])
        for i, (src, dst) in enumerate(
            [
                (q_hbm, qv),
                (nk_hbm, nkv),
                (nv_hbm, nvv),
                (gain_hbm, gains.at[me]),
                (hidden_hbm, hid),
                (ck_hbm, ck),
                (cv_hbm, cv),
            ]
        )
    ]
    for c in ins:
        c.start()

    DB = wo_hbm.shape[2]
    ROWS, VL = ring.shape[1], ring.shape[2]
    per = VL // DB
    KO = wo_hbm.shape[1]
    pieces = KO // ROWS
    held_slots = pieces // per
    wo_places = [
        (NBUF - held_slots + i // per, (i % per) * DB, i * ROWS) for i in range(pieces)
    ]
    wo_copies = [
        pltpu.make_async_copy(
            wo_hbm.at[0, pl.ds(row, ROWS), :],
            ring.at[slot, :, pl.ds(lane, DB)],
            wo_sem.at[i],
        )
        for i, (slot, lane, row) in enumerate(wo_places)
    ]
    for c in wo_copies:
        c.start()

    def block_of(o):
        return lax.rem(p * QUAD + o, NCH)

    def lm_copy(o, slot):
        row = pl.multiple_of(block_of(o) * ROWS, ROWS)
        return pltpu.make_async_copy(
            lm_hbm.at[pl.ds(row, ROWS), :], ring.at[slot], ring_sem.at[slot]
        )

    free = NBUF - held_slots

    def start_chunks(first, last):
        for o in range(min(first, free), min(last, free)):
            lm_copy(o, o).start()

    start_chunks(0, 2)

    for c in ins[:4]:
        c.wait()
    for j in range(QL):
        stage[j * S : (j + 1) * S, :] = qv[:, j * HD : (j + 1) * HD].astype(F32)
    for j in range(KV):
        stage[(QL + j) * S : (QL + j + 1) * S, :] = nkv[:, j * HD : (j + 1) * HD].astype(F32)
        stage[(QL + KV + j) * S : (QL + KV + j + 1) * S, :] = nvv[
            :, j * HD : (j + 1) * HD
        ].astype(F32)
    xq[p] = stage[...].astype(BF)

    pl.semaphore_wait(barrier, len(everyone))

    def send(src, dst, ssem, rsem, to):
        c = pltpu.make_async_remote_copy(
            src_ref=src, dst_ref=dst, send_sem=ssem, recv_sem=rsem,
            device_id=to, device_id_type=MESH,
        )
        c.start()
        return c

    sent = []
    q_copies = [
        send(xq.at[p], xq.at[p], q_send.at[d], q_recv.at[d], at(d, 0, 0))
        for d in range(1, NP)
    ]
    sent += q_copies
    for i, d in enumerate(everyone):
        sent.append(send(gains.at[me], gains.at[me], g_send.at[i], g_recv.at[me], at(*d)))

    slots = [slot_ref[r] for r in range(R)]
    lengths = [len_ref[r] for r in range(R)]
    rows_q = iota((S * QL, NP * QL * S), 0)
    cols_q = iota((S * QL, NP * QL * S), 1)
    req_q = (cols_q // (QL * S)) * S + cols_q % S
    hot_q = jnp.where(
        ((cols_q // S) % QL == rows_q % QL) & (pick(req_q, slots) == p * S + rows_q // QL),
        1.0,
        0.0,
    ).astype(BF)
    M2 = 2 * KV * S
    rows_k = iota((2 * S * QL, NP * M2), 0)
    cols_k = iota((2 * S * QL, NP * M2), 1)
    req_k = (cols_k // M2) * S + cols_k % S
    hot_k = jnp.where(
        ((cols_k // S) % (2 * KV) == (rows_k // (S * QL)) * KV + (rows_k % QL) // G)
        & (pick(req_k, slots) == p * S + (rows_k % (S * QL)) // QL),
        1.0,
        0.0,
    ).astype(BF)
    position = h * SPAN + iota((G, SPAN), 1)
    live = []
    for s in range(S):
        length = jnp.int32(0)
        for r in range(R):
            length = length + jnp.where(slots[r] == p * S + s, lengths[r], 0)
        live.append(position < length)

    for c in q_copies:
        c.wait_recv()
    start_chunks(2, 6)
    Xq = xq[:, 0 : QL * S, :].reshape(NP * QL * S, HD)
    Xk = xq[:, QL * S :, :].reshape(NP * M2, HD)
    Qs = mm(hot_q, Xq)
    KVs = mm(hot_k, Xk)
    own = jnp.exp(jnp.sum(Qs * KVs[: S * QL], axis=1, keepdims=True) * scale)
    own = own * jnp.where(h == 0, 1.0, 0.0)

    for c in ins[5:]:
        c.wait()
    total_parts, mixed_parts = [], []
    for s in range(S):
        for k in range(KV):
            at_row = (s * KV + k) * G
            query = Qs[at_row : at_row + G].astype(BF)
            scores = lax.dot_general(
                query,
                ck[s, :, k * HD : (k + 1) * HD],
                (((1,), (1,)), ((), ())),
                preferred_element_type=F32,
            )
            weights = jnp.where(live[s], jnp.exp(scores * scale), 0.0)
            total_parts.append(jnp.sum(weights, axis=1, keepdims=True))
            mixed_parts.append(mm(weights.astype(BF), cv[s, :, k * HD : (k + 1) * HD]))
    total = jnp.concatenate(total_parts, axis=0) + own
    mixed = jnp.concatenate(mixed_parts, axis=0) + own * KVs[S * QL :]
    B = S * HO
    diag = iota((B, HD), 0) == iota((B, HD), 1)
    lines = iota((16, HD), 0)
    for t in range(NH):
        column = []
        for s in range(S):
            first = s * QL + t * HO
            send2[t, s * HO : (s + 1) * HO, :] = mixed[first : first + HO].astype(BF)
            column.append(total[first : first + HO])
        column = jnp.concatenate(column, axis=0)
        line = jnp.sum(jnp.where(diag, column, 0.0), axis=0, keepdims=True)
        high = line.astype(BF).astype(F32)
        send2[t, B:, :] = jnp.where(
            lines == 0, high, jnp.where(lines == 1, line - high, 0.0)
        ).astype(BF)
    here = p * NH + h
    recv2[here] = send2[h]
    a_copies = []
    for i, (dp, dh, da) in enumerate([d for d in everyone if d[2] == 0]):
        to = at(dp, dh, 0)
        a_copies.append(
            send(send2.at[to["head"]], recv2.at[here], a_send.at[i], a_recv.at[i], to)
        )
    sent += a_copies

    RH = iota((HO * R, NP * B), 0)
    CH = iota((HO * R, NP * B), 1)
    order = jnp.where(
        (RH // R == CH % HO) & (pick(RH % R, slots) == CH // HO), 1.0, 0.0
    ).astype(BF)
    for c in a_copies:
        c.wait_recv()
    start_chunks(6, 10)
    attended = []
    for q in range(NP):
        got = recv2[q * NH].astype(F32)
        for t in range(1, NH):
            got = got + recv2[q * NH + t].astype(F32)
        line = got[B : B + 1] + got[B + 1 : B + 2]
        column = jnp.sum(jnp.where(diag, line, 0.0), axis=1, keepdims=True)
        attended.append((got[:B] / column).astype(BF))
    by_head = mm(order, jnp.concatenate(attended, axis=0))
    by_request = jnp.concatenate(
        [by_head[j * R : (j + 1) * R] for j in range(HO)], axis=1
    ).astype(BF)

    for c in wo_copies:
        c.wait()
    mine = h * NA + a
    for n in range(QUAD):
        term = jnp.zeros((R, W), F32)
        for slot, lane, row in wo_places:
            term = term + mm(
                by_request[:, row : row + ROWS], ring[slot, :, lane + n * W : lane + (n + 1) * W]
            )
        send3[n] = term
    recv3[mine] = send3[mine]
    t_copies = []
    for i, (dp, dh, da) in enumerate([d for d in everyone if d[0] == 0]):
        to = at(0, dh, da)
        t_copies.append(
            send(
                send3.at[to["head"] * NA + to["aux"]],
                recv3.at[mine],
                t_send.at[i],
                t_recv.at[i],
                to,
            )
        )
    sent += t_copies
    ins[4].wait()
    for c in t_copies:
        c.wait_recv()
    stream = hid[...].astype(F32)
    projected = recv3[0]
    for n in range(1, QUAD):
        projected = projected + recv3[n]
    stream = stream + projected
    xs[me] = jnp.concatenate([stream[:, : W // 2], stream[:, W // 2 :]], axis=0).astype(BF)
    for i, d in enumerate(everyone):
        sent.append(send(xs.at[me], xs.at[me], s_send.at[i], s_recv.at[me], at(*d)))
    start_chunks(10, free)
    for o in range(free, NBUF):
        lm_copy(o, o).start()

    acc[...] = jnp.zeros_like(acc)

    def step(o, squares):
        b = block_of(o)
        slot = lax.rem(o, NBUF)

        @pl.when(b != me)
        def _():
            pltpu.make_async_remote_copy(
                src_ref=gains.at[b], dst_ref=gains.at[b], send_sem=g_send.at[0],
                recv_sem=g_recv.at[b], device_id=at(1, 0, 0), device_id_type=MESH,
            ).wait_recv()
            pltpu.make_async_remote_copy(
                src_ref=xs.at[b], dst_ref=xs.at[b], send_sem=s_send.at[0],
                recv_sem=s_recv.at[b], device_id=at(1, 0, 0), device_id_type=MESH,
            ).wait_recv()

        halves = xs[b].astype(F32)
        block = jnp.concatenate([halves[:R], halves[R:]], axis=1)
        left = (block * gains[b]).astype(BF)
        lm_copy(o, slot).wait()
        acc[...] += mm(left, ring[slot])

        @pl.when(o + NBUF < NCH)
        def _():
            lm_copy(o + NBUF, slot).start()

        return squares + jnp.sum(block * block, axis=1, keepdims=True)

    squares = lax.fori_loop(0, NCH, step, jnp.zeros((R, 1), F32))
    logits = acc[...] * lax.rsqrt(squares * (1.0 / (NCH * ROWS)) + 1e-05)
    acc[...] = logits
    out = pltpu.make_async_copy(acc, logits_hbm, out_sem)
    out.start()
    expd = jnp.exp(logits)
    sums = jnp.sum(expd, axis=1, keepdims=True)
    moments = jnp.sum(expd * logits, axis=1, keepdims=True)
    lane = iota((R, HD), 1)
    xe[me] = jnp.where(lane == 0, sums, jnp.where(lane == 1, moments, 0.0))
    e_copies = [
        send(xe.at[me], xe.at[me], e_send.at[i], e_recv.at[i], at(*d))
        for i, d in enumerate(everyone)
    ]
    sent += e_copies
    for c in e_copies:
        c.wait_recv()
    both = jnp.sum(xe[...], axis=0)
    vocab_total, moment = both[:, 0:1], both[:, 1:2]
    entropy = jnp.log(vocab_total) - moment / vocab_total
    spread = jnp.sum(jnp.where(iota((R, HD), 0) == lane, entropy, 0.0), axis=0, keepdims=True)
    ent_ref[...] = spread[:, :R]
    out.wait()
    for c in sent:
        c.wait_send()


def closing(logits_in, ent_in, logits_out, ent_out, sem):
    copy = pltpu.make_async_copy(logits_in, logits_out, sem)
    copy.start()
    ent_out[...] = ent_in[...]
    copy.wait()


def one_kernel(
    cfg,
    hidden, gain, queries, new_key, new_value, cache_key, cache_value, lengths, slot_of,
    out_proj, lm_head,
):
    NP, NH, NA = cfg["NP"], cfg["NH"], cfg["NA"]
    R, S, KV, G, SPAN = cfg["R"], cfg["S"], cfg["KV"], cfg["G"], cfg["SPAN"]
    W, NCH, NBUF = cfg["W"], cfg["NCH"], cfg["NBUF"]
    QL = KV * G
    N = NP * NH * NA
    QUAD = NH * NA
    VL = lm_head.shape[1]
    rows = (QL + 2 * KV) * S
    message = S * (QL // NH) + 16
    DMA = pltpu.SemaphoreType.DMA
    smem = pl.BlockSpec(memory_space=pltpu.SMEM)
    anywhere = pl.BlockSpec(memory_space=pl.ANY)
    weights = lm_head.size + out_proj.size + 2 * cache_key.size
    logits, entropy = pl.pallas_call(
        functools.partial(kernel, cfg),
        out_shape=(
            jax.ShapeDtypeStruct((R, VL), F32),
            jax.ShapeDtypeStruct((1, R), F32),
        ),
        in_specs=[smem, smem] + [anywhere] * 9,
        out_specs=(anywhere, pl.BlockSpec(memory_space=pltpu.VMEM)),
        scratch_shapes=[
            pltpu.VMEM((NBUF, W, VL), BF),
            pltpu.VMEM(cache_key.shape, BF),
            pltpu.VMEM(cache_value.shape, BF),
            pltpu.VMEM(queries.shape, BF),
            pltpu.VMEM(new_key.shape, BF),
            pltpu.VMEM(new_value.shape, BF),
            pltpu.VMEM(hidden.shape, BF),
            pltpu.VMEM((N, 1, W), F32),
            pltpu.VMEM((rows, HD), F32),
            pltpu.VMEM((NP, rows, HD), BF),
            pltpu.VMEM((NH, message, HD), BF),
            pltpu.VMEM((NP * NH, message, HD), BF),
            pltpu.VMEM((QUAD, R, W), F32),
            pltpu.VMEM((QUAD, R, W), F32),
            pltpu.VMEM((N, 2 * R, W // 2), BF),
            pltpu.VMEM((R, VL), F32),
            pltpu.VMEM((N, R, HD), F32),
            DMA((NBUF,)),
            DMA((out_proj.shape[1] // W,)),
            DMA((7,)),
            DMA,
            DMA((NP,)),
            DMA((NP,)),
            DMA((N,)),
            DMA((N,)),
            DMA((NP * NH,)),
            DMA((NP * NH,)),
            DMA((QUAD,)),
            DMA((QUAD,)),
            DMA((N,)),
            DMA((N,)),
            DMA((N,)),
            DMA((N,)),
        ],
        compiler_params=pltpu.CompilerParams(
            collective_id=0, has_side_effects=True, vmem_limit_bytes=63 * MIB
        ),
        cost_estimate=pl.CostEstimate(
            flops=2 * R * weights, bytes_accessed=2 * weights, transcendentals=R * VL
        ),
    )(
        slot_of, lengths, hidden, gain.reshape(1, W), queries, new_key, new_value,
        cache_key, cache_value, out_proj, lm_head,
    )
    logits, entropy = pl.pallas_call(
        closing,
        out_shape=(
            jax.ShapeDtypeStruct((R, VL), F32),
            jax.ShapeDtypeStruct((1, R), F32),
        ),
        in_specs=[anywhere, pl.BlockSpec(memory_space=pltpu.VMEM)],
        out_specs=(anywhere, pl.BlockSpec(memory_space=pltpu.VMEM)),
        scratch_shapes=[DMA],
    )(logits, entropy)
    return logits, entropy.reshape(R)


def arrangement(mesh, args):
    NP, NH, NA = mesh.shape["pool"], mesh.shape["head"], mesh.shape["aux"]
    hidden, queries, cache_key, out_proj, lm_head = (
        args[0], args[2], args[5], args[9], args[10],
    )
    R, W = hidden.shape
    S, SPAN = cache_key.shape[:2]
    KV = cache_key.shape[2] // HD
    QL = queries.shape[1] // HD
    VL = lm_head.shape[1]
    HO = out_proj.shape[1] // HD
    fits = (
        R == 8
        and W % 256 == 0
        and VL % out_proj.shape[2] == 0
        and out_proj.shape[1] % W == 0
        and (out_proj.shape[1] // W) % (VL // out_proj.shape[2]) == 0
        and HO % 16 == 0
        and S * HO <= HD
        and QL // KV == 8
        and (KV * S) % 8 == 0
        and SPAN % 128 == 0
        and W * VL * 2 * RING <= 60 * MIB
    )
    if not fits:
        return None
    return dict(
        NP=NP, NH=NH, NA=NA, R=R, S=S, KV=KV, G=QL // KV, SPAN=SPAN, W=W,
        NCH=lm_head.shape[0] // W, NBUF=min(RING, lm_head.shape[0] // W),
    )


def select_rows(onehot, rows):
    return jnp.dot(onehot.astype(jnp.bfloat16), rows, preferred_element_type=jnp.float32).astype(
        jnp.bfloat16
    )


def per_device(
    hidden,
    gain,
    queries,
    new_key,
    new_value,
    cache_key,
    cache_value,
    lengths,
    slot_of,
    out_proj,
    lm_head,
):
    slots_here = cache_key.shape[0]
    span = cache_key.shape[1]
    kv_here = cache_key.shape[2] // HD
    q_here = queries.shape[1] // HD
    group = q_here // kv_here
    heads_out = out_proj.shape[1] // HD
    scale = 1.0 / math.sqrt(HD)
    pool_place = lax.axis_index("pool")
    head_place = lax.axis_index("head")
    all_queries, all_keys, all_values = (
        lax.all_gather(queries, "pool", axis=0, tiled=True),
        lax.all_gather(new_key, "pool", axis=0, tiled=True),
        lax.all_gather(new_value, "pool", axis=0, tiled=True),
    )
    requests = all_queries.shape[0]
    slot_ids = pool_place * slots_here + jnp.arange(slots_here, dtype=jnp.int32)
    chosen = slot_of[None, :] == slot_ids[:, None]
    query_slot = select_rows(chosen, all_queries)
    key_slot = select_rows(chosen, all_keys)
    value_slot = select_rows(chosen, all_values)
    length_slot = jnp.sum(jnp.where(chosen, lengths[None, :], 0), axis=1)
    query_heads = query_slot.reshape(slots_here, kv_here, group, HD)
    keys = cache_key.reshape(slots_here, span, kv_here, HD)
    values = cache_value.reshape(slots_here, span, kv_here, HD)
    scores = (
        jnp.einsum("skgd,stkd->skgt", query_heads, keys, preferred_element_type=jnp.float32) * scale
    )
    position = head_place * span + jnp.arange(span, dtype=jnp.int32)
    live = position[None, :] < length_slot[:, None]
    weights = jnp.where(live[:, None, None, :], jnp.exp(scores), 0.0)
    total = jnp.sum(weights, axis=3).reshape(slots_here, q_here)
    mixed = jnp.einsum(
        "skgt,stkd->skgd", weights.astype(jnp.bfloat16), values, preferred_element_type=jnp.float32
    )
    mixed = mixed.reshape(slots_here, q_here * HD)
    total, mixed = (
        lax.psum(total.astype(jnp.bfloat16), "head").astype(jnp.float32),
        lax.psum(mixed.astype(jnp.bfloat16), "head").astype(jnp.float32),
    )
    total = lax.dynamic_slice_in_dim(total, head_place * heads_out, heads_out, 1)
    mixed = lax.dynamic_slice_in_dim(mixed, head_place * heads_out * HD, heads_out * HD, 1)
    query_own = lax.dynamic_slice_in_dim(query_slot, head_place * heads_out * HD, heads_out * HD, 1)
    query_own = query_own.reshape(slots_here, heads_out, HD).astype(jnp.float32)
    key_spread = jnp.repeat(key_slot.reshape(slots_here, kv_here, HD), group, axis=1)
    value_spread = jnp.repeat(value_slot.reshape(slots_here, kv_here, HD), group, axis=1)
    key_own = lax.dynamic_slice_in_dim(key_spread, head_place * heads_out, heads_out, 1).astype(
        jnp.float32
    )
    value_own = lax.dynamic_slice_in_dim(value_spread, head_place * heads_out, heads_out, 1).astype(
        jnp.float32
    )
    own = jnp.exp(jnp.sum(query_own * key_own, axis=2) * scale)
    total = total + own
    mixed = mixed.reshape(slots_here, heads_out, HD) + own[:, :, None] * value_own
    attended = (mixed / total[:, :, None]).astype(jnp.bfloat16).reshape(slots_here, heads_out * HD)
    outputs = lax.all_gather(attended, "pool", axis=0, tiled=True)
    order = slot_of[:, None] == jnp.arange(requests, dtype=jnp.int32)[None, :]
    by_request = select_rows(order, outputs)
    weight_block = out_proj[0]
    term = jnp.dot(by_request, weight_block, preferred_element_type=jnp.float32)
    projected = lax.psum(term.astype(jnp.bfloat16), ("head", "aux")).astype(jnp.float32)
    block_hidden, block_gain = (
        lax.all_gather(hidden, ("head", "aux"), axis=1, tiled=True),
        lax.all_gather(gain.astype(jnp.bfloat16), ("head", "aux"), axis=0, tiled=True).astype(
            gain.dtype
        ),
    )
    stream = (block_hidden.astype(jnp.float32) + projected).astype(jnp.bfloat16)
    full_stream, full_gain = (
        lax.all_gather(stream, "pool", axis=1, tiled=True),
        lax.all_gather(block_gain.astype(jnp.bfloat16), "pool", axis=0, tiled=True).astype(
            block_gain.dtype
        ),
    )
    stream_wide = full_stream.astype(jnp.float32)
    mean_sq = jnp.mean(stream_wide * stream_wide, axis=1, keepdims=True)
    normed = (stream_wide * lax.rsqrt(mean_sq + 1e-05) * full_gain[None, :]).astype(jnp.bfloat16)
    logits = jnp.dot(normed, lm_head, preferred_element_type=jnp.float32)
    expd = jnp.exp(logits)
    vocab_total, moment = lax.psum(
        (jnp.sum(expd, axis=1), jnp.sum(expd * logits, axis=1)), ("pool", "head", "aux")
    )
    entropy = jnp.log(vocab_total) - moment / vocab_total
    return (logits, entropy)


def solution(mesh):
    in_specs = (
        P("grp", ("pool", "head", "aux")),
        P(("pool", "head", "aux")),
        P(("grp", "pool"), "aux"),
        P(("grp", "pool"), "aux"),
        P(("grp", "pool"), "aux"),
        P(("grp", "pool"), "head", "aux"),
        P(("grp", "pool"), "head", "aux"),
        P("grp"),
        P("grp"),
        P("aux", "head", "pool"),
        P(None, ("pool", "head", "aux")),
    )
    out_specs = (P("grp", ("pool", "head", "aux")), P("grp"))

    def on_device(*args):
        cfg = arrangement(mesh, args)
        if cfg is None:
            return per_device(*args)
        return one_kernel(cfg, *args)

    return jax.shard_map(
        on_device, mesh=mesh, in_specs=in_specs, out_specs=out_specs, check_vma=False
    )
```

```python
import functools
import math

import jax
import jax.numpy as jnp
from jax import lax
from jax.experimental import pallas as pl
from jax.experimental.pallas import tpu as pltpu
from jax.sharding import PartitionSpec as P

HD = 128
MESH = pl.DeviceIdType.MESH
BF = jnp.bfloat16
F32 = jnp.float32
MIB = 1024 * 1024
RING = 15


def iota(shape, axis):
    return lax.broadcasted_iota(jnp.int32, shape, axis)


def mm(a, b):
    return jnp.dot(a, b, preferred_element_type=F32)


def pick(position, scalars):
    out = jnp.full(position.shape, scalars[0], jnp.int32)
    for r in range(1, len(scalars)):
        out = jnp.where(position == r, scalars[r], out)
    return out


def kernel(
    cfg,
    slot_ref,
    len_ref,
    hidden_hbm,
    gain_hbm,
    q_hbm,
    nk_hbm,
    nv_hbm,
    ck_hbm,
    cv_hbm,
    wo_hbm,
    lm_hbm,
    logits_hbm,
    ent_ref,
    ring,
    ck,
    cv,
    qv,
    nkv,
    nvv,
    hid,
    gains,
    stage,
    xq,
    send2,
    recv2,
    send3,
    recv3,
    xs,
    lefts,
    acc,
    xe,
    ring_sem,
    wo_sem,
    in_sem,
    out_sem,
    q_send,
    q_recv,
    g_send,
    g_recv,
    a_send,
    a_recv,
    t_send,
    t_recv,
    s_send,
    s_recv,
    e_send,
    e_recv,
):
    NP, NH, NA = cfg["NP"], cfg["NH"], cfg["NA"]
    R, S, KV, G, SPAN = cfg["R"], cfg["S"], cfg["KV"], cfg["G"], cfg["SPAN"]
    W, NCH, NBUF = cfg["W"], cfg["NCH"], cfg["NBUF"]
    QL = KV * G
    HO = QL // NH
    QUAD = NH * NA
    scale = 1.0 / math.sqrt(HD)
    p = lax.axis_index("pool")
    h = lax.axis_index("head")
    a = lax.axis_index("aux")
    me = (p * NH + h) * NA + a
    everyone = [
        (dp, dh, da)
        for dp in range(NP)
        for dh in range(NH)
        for da in range(NA)
        if (dp, dh, da) != (0, 0, 0)
    ]

    def at(dp, dh, da):
        return {
            "pool": lax.rem(p + dp, NP),
            "head": lax.rem(h + dh, NH),
            "aux": lax.rem(a + da, NA),
        }

    def place(where):
        return (where["pool"] * NH + where["head"]) * NA + where["aux"]

    barrier = pltpu.get_barrier_semaphore()
    for d in everyone:
        pl.semaphore_signal(barrier, inc=1, device_id=at(*d), device_id_type=MESH)

    ins = [
        pltpu.make_async_copy(src, dst, in_sem.at[i])
        for i, (src, dst) in enumerate(
            [
                (q_hbm, qv),
                (nk_hbm, nkv),
                (nv_hbm, nvv),
                (gain_hbm, gains.at[me]),
                (hidden_hbm, hid),
                (ck_hbm, ck),
                (cv_hbm, cv),
            ]
        )
    ]
    for c in ins:
        c.start()

    DB = wo_hbm.shape[2]
    ROWS, VL = ring.shape[1], ring.shape[2]
    per = VL // DB
    KO = wo_hbm.shape[1]
    pieces = KO // ROWS
    held_slots = pieces // per
    wo_places = [
        (NBUF - held_slots + i // per, (i % per) * DB, i * ROWS) for i in range(pieces)
    ]
    wo_copies = [
        pltpu.make_async_copy(
            wo_hbm.at[0, pl.ds(row, ROWS), :],
            ring.at[slot, :, pl.ds(lane, DB)],
            wo_sem.at[i],
        )
        for i, (slot, lane, row) in enumerate(wo_places)
    ]
    for c in wo_copies:
        c.start()

    def block_of(o):
        return lax.rem(p * QUAD + o, NCH)

    def lm_copy(o, slot):
        row = pl.multiple_of(block_of(o) * ROWS, ROWS)
        return pltpu.make_async_copy(
            lm_hbm.at[pl.ds(row, ROWS), :], ring.at[slot], ring_sem.at[slot]
        )

    free = NBUF - held_slots

    def start_chunks(first, last):
        for o in range(min(first, free), min(last, free)):
            lm_copy(o, o).start(priority=1)

    start_chunks(0, 2)

    for c in ins[:4]:
        c.wait()
    for j in range(QL):
        stage[j * S : (j + 1) * S, :] = qv[:, j * HD : (j + 1) * HD].astype(F32)
    for j in range(KV):
        stage[(QL + j) * S : (QL + j + 1) * S, :] = nkv[:, j * HD : (j + 1) * HD].astype(F32)
        stage[(QL + KV + j) * S : (QL + KV + j + 1) * S, :] = nvv[
            :, j * HD : (j + 1) * HD
        ].astype(F32)
    xq[p] = stage[...].astype(BF)

    pl.semaphore_wait(barrier, len(everyone))

    def send(src, dst, ssem, rsem, to):
        c = pltpu.make_async_remote_copy(
            src_ref=src, dst_ref=dst, send_sem=ssem, recv_sem=rsem,
            device_id=to, device_id_type=MESH,
        )
        c.start()
        return c

    sent = []
    q_copies = [
        send(xq.at[p], xq.at[p], q_send.at[d], q_recv.at[d], at(d, 0, 0))
        for d in range(1, NP)
    ]
    sent += q_copies
    for i, d in enumerate(everyone):
        sent.append(send(gains.at[me], gains.at[me], g_send.at[i], g_recv.at[me], at(*d)))
    start_chunks(2, 4)

    slots = [slot_ref[r] for r in range(R)]
    lengths = [len_ref[r] for r in range(R)]
    rows_q = iota((S * QL, NP * QL * S), 0)
    cols_q = iota((S * QL, NP * QL * S), 1)
    req_q = (cols_q // (QL * S)) * S + cols_q % S
    hot_q = jnp.where(
        ((cols_q // S) % QL == rows_q % QL) & (pick(req_q, slots) == p * S + rows_q // QL),
        1.0,
        0.0,
    ).astype(BF)
    M2 = 2 * KV * S
    rows_k = iota((2 * S * QL, NP * M2), 0)
    cols_k = iota((2 * S * QL, NP * M2), 1)
    req_k = (cols_k // M2) * S + cols_k % S
    hot_k = jnp.where(
        ((cols_k // S) % (2 * KV) == (rows_k // (S * QL)) * KV + (rows_k % QL) // G)
        & (pick(req_k, slots) == p * S + (rows_k % (S * QL)) // QL),
        1.0,
        0.0,
    ).astype(BF)
    position = h * SPAN + iota((G, SPAN), 1)
    live = []
    for s in range(S):
        length = jnp.int32(0)
        for r in range(R):
            length = length + jnp.where(slots[r] == p * S + s, lengths[r], 0)
        live.append(position < length)

    for c in q_copies:
        c.wait_recv()
    Xq = xq[:, 0 : QL * S, :].reshape(NP * QL * S, HD)
    Xk = xq[:, QL * S :, :].reshape(NP * M2, HD)
    Qs = mm(hot_q, Xq)
    KVs = mm(hot_k, Xk)
    own = jnp.exp(jnp.sum(Qs * KVs[: S * QL], axis=1, keepdims=True) * scale)
    own = own * jnp.where(h == 0, 1.0, 0.0)

    for c in ins[5:]:
        c.wait()
    total_parts, mixed_parts = [], []
    for s in range(S):
        for k in range(KV):
            at_row = (s * KV + k) * G
            query = Qs[at_row : at_row + G].astype(BF)
            scores = lax.dot_general(
                query,
                ck[s, :, k * HD : (k + 1) * HD],
                (((1,), (1,)), ((), ())),
                preferred_element_type=F32,
            )
            weights = jnp.where(live[s], jnp.exp(scores * scale), 0.0)
            total_parts.append(jnp.sum(weights, axis=1, keepdims=True))
            mixed_parts.append(mm(weights.astype(BF), cv[s, :, k * HD : (k + 1) * HD]))
    total = jnp.concatenate(total_parts, axis=0) + own
    mixed = jnp.concatenate(mixed_parts, axis=0) + own * KVs[S * QL :]
    B = S * HO
    diag = iota((B, HD), 0) == iota((B, HD), 1)
    lines = iota((16, HD), 0)
    for t in range(NH):
        column = []
        for s in range(S):
            first = s * QL + t * HO
            send2[t, s * HO : (s + 1) * HO, :] = mixed[first : first + HO].astype(BF)
            column.append(total[first : first + HO])
        column = jnp.concatenate(column, axis=0)
        line = jnp.sum(jnp.where(diag, column, 0.0), axis=0, keepdims=True)
        high = line.astype(BF).astype(F32)
        send2[t, B:, :] = jnp.where(
            lines == 0, high, jnp.where(lines == 1, line - high, 0.0)
        ).astype(BF)
    here = p * NH + h
    recv2[here] = send2[h]
    a_copies = []
    for i, (dp, dh, da) in enumerate([d for d in everyone if d[2] == 0]):
        to = at(dp, dh, 0)
        a_copies.append(
            send(send2.at[to["head"]], recv2.at[here], a_send.at[i], a_recv.at[i], to)
        )
    sent += a_copies
    start_chunks(4, 6)

    RH = iota((HO * R, NP * B), 0)
    CH = iota((HO * R, NP * B), 1)
    order = jnp.where(
        (RH // R == CH % HO) & (pick(RH % R, slots) == CH // HO), 1.0, 0.0
    ).astype(BF)
    for c in a_copies:
        c.wait_recv()
    attended = []
    for q in range(NP):
        got = recv2[q * NH].astype(F32)
        for t in range(1, NH):
            got = got + recv2[q * NH + t].astype(F32)
        line = got[B : B + 1] + got[B + 1 : B + 2]
        column = jnp.sum(jnp.where(diag, line, 0.0), axis=1, keepdims=True)
        attended.append((got[:B] / column).astype(BF))
    by_head = mm(order, jnp.concatenate(attended, axis=0))
    by_request = jnp.concatenate(
        [by_head[j * R : (j + 1) * R] for j in range(HO)], axis=1
    ).astype(BF)

    for c in wo_copies:
        c.wait()
    mine = h * NA + a
    t_copies = []
    for i in range(1, QUAD + 1):
        n = lax.rem(mine + i, QUAD)
        term = jnp.zeros((R, W), F32)
        for slot, lane, row in wo_places:
            part = pl.ds(pl.multiple_of(lane + n * W, W), W)
            term = term + mm(by_request[:, row : row + ROWS], ring[slot, :, part])
        if i == QUAD:
            recv3[mine] = term
        else:
            send3[n] = term
            to = {"pool": p, "head": n // NA, "aux": lax.rem(n, NA)}
            t_copies.append(
                send(send3.at[n], recv3.at[mine], t_send.at[i], t_recv.at[i], to)
            )
            if i == QUAD - 1:
                start_chunks(6, 8)
    sent += t_copies
    ins[4].wait()
    for c in t_copies:
        c.wait_recv()
    stream = hid[...].astype(F32)
    projected = recv3[0]
    for n in range(1, QUAD):
        projected = projected + recv3[n]
    stream = stream + projected
    xs[me] = jnp.concatenate([stream[:, : W // 2], stream[:, W // 2 :]], axis=0).astype(BF)
    for i, d in enumerate(everyone):
        sent.append(send(xs.at[me], xs.at[me], s_send.at[i], s_recv.at[me], at(*d)))
    start_chunks(8, free)
    for o in range(free, NBUF):
        lm_copy(o, o).start(priority=1)

    acc[...] = jnp.zeros_like(acc)

    def arrived(block, sems):
        return pltpu.make_async_remote_copy(
            src_ref=block, dst_ref=block, send_sem=s_send.at[0], recv_sem=sems,
            device_id=at(1, 0, 0), device_id_type=MESH,
        )

    def group(g, squares):
        for i in range(QUAD):
            b = block_of(g * QUAD + i)

            @pl.when(b != me)
            def _():
                arrived(gains.at[b], g_recv.at[b]).wait_recv()
                arrived(xs.at[b], s_recv.at[b]).wait_recv()

        for i in range(QUAD):
            b = block_of(g * QUAD + i)
            halves = xs[b].astype(F32)
            block = jnp.concatenate([halves[:R], halves[R:]], axis=1)
            lefts[i] = (block * gains[b]).astype(BF)
            squares = squares + jnp.sum(block * block, axis=1, keepdims=True)

        def step(i, none):
            o = g * QUAD + i
            slot = lax.rem(o, NBUF)
            lm_copy(o, slot).wait()
            acc[...] += mm(lefts[i], ring[slot])

            @pl.when(o + NBUF < NCH)
            def _():
                lm_copy(o + NBUF, slot).start(priority=1)

            return none

        lax.fori_loop(0, QUAD, step, 0)
        return squares

    squares = lax.fori_loop(0, NCH // QUAD, group, jnp.zeros((R, 1), F32))
    logits = acc[...] * lax.rsqrt(squares * (1.0 / (NCH * ROWS)) + 1e-05)
    acc[...] = logits
    out = pltpu.make_async_copy(acc, logits_hbm, out_sem)
    out.start()
    expd = jnp.exp(logits)
    sums = jnp.sum(expd, axis=1, keepdims=True)
    moments = jnp.sum(expd * logits, axis=1, keepdims=True)
    lane = iota((R, HD), 1)
    xe[me] = jnp.where(lane == 0, sums, jnp.where(lane == 1, moments, 0.0))
    e_copies = [
        send(xe.at[me], xe.at[me], e_send.at[i], e_recv.at[i], at(*d))
        for i, d in enumerate(everyone)
    ]
    sent += e_copies
    for c in e_copies:
        c.wait_recv()
    both = jnp.sum(xe[...], axis=0)
    vocab_total, moment = both[:, 0:1], both[:, 1:2]
    entropy = jnp.log(vocab_total) - moment / vocab_total
    spread = jnp.sum(jnp.where(iota((R, HD), 0) == lane, entropy, 0.0), axis=0, keepdims=True)
    ent_ref[...] = spread[:, :R]
    out.wait()
    for c in sent:
        c.wait_send()


def closing(logits_in, ent_in, logits_out, ent_out, sem):
    copy = pltpu.make_async_copy(logits_in, logits_out, sem)
    copy.start()
    ent_out[...] = ent_in[...]
    copy.wait()


def one_kernel(
    cfg,
    hidden, gain, queries, new_key, new_value, cache_key, cache_value, lengths, slot_of,
    out_proj, lm_head,
):
    NP, NH, NA = cfg["NP"], cfg["NH"], cfg["NA"]
    R, S, KV, G, SPAN = cfg["R"], cfg["S"], cfg["KV"], cfg["G"], cfg["SPAN"]
    W, NCH, NBUF = cfg["W"], cfg["NCH"], cfg["NBUF"]
    QL = KV * G
    N = NP * NH * NA
    QUAD = NH * NA
    VL = lm_head.shape[1]
    rows = (QL + 2 * KV) * S
    message = S * (QL // NH) + 16
    DMA = pltpu.SemaphoreType.DMA
    smem = pl.BlockSpec(memory_space=pltpu.SMEM)
    anywhere = pl.BlockSpec(memory_space=pl.ANY)
    weights = lm_head.size + out_proj.size + 2 * cache_key.size
    logits, entropy = pl.pallas_call(
        functools.partial(kernel, cfg),
        out_shape=(
            jax.ShapeDtypeStruct((R, VL), F32),
            jax.ShapeDtypeStruct((1, R), F32),
        ),
        in_specs=[smem, smem] + [anywhere] * 9,
        out_specs=(anywhere, pl.BlockSpec(memory_space=pltpu.VMEM)),
        scratch_shapes=[
            pltpu.VMEM((NBUF, W, VL), BF),
            pltpu.VMEM(cache_key.shape, BF),
            pltpu.VMEM(cache_value.shape, BF),
            pltpu.VMEM(queries.shape, BF),
            pltpu.VMEM(new_key.shape, BF),
            pltpu.VMEM(new_value.shape, BF),
            pltpu.VMEM(hidden.shape, BF),
            pltpu.VMEM((N, 1, W), F32),
            pltpu.VMEM((rows, HD), F32),
            pltpu.VMEM((NP, rows, HD), BF),
            pltpu.VMEM((NH, message, HD), BF),
            pltpu.VMEM((NP * NH, message, HD), BF),
            pltpu.VMEM((QUAD, R, W), F32),
            pltpu.VMEM((QUAD, R, W), F32),
            pltpu.VMEM((N, 2 * R, W // 2), BF),
            pltpu.VMEM((QUAD, R, W), BF),
            pltpu.VMEM((R, VL), F32),
            pltpu.VMEM((N, R, HD), F32),
            DMA((NBUF,)),
            DMA((out_proj.shape[1] // W,)),
            DMA((7,)),
            DMA,
            DMA((NP,)),
            DMA((NP,)),
            DMA((N,)),
            DMA((N,)),
            DMA((NP * NH,)),
            DMA((NP * NH,)),
            DMA((QUAD,)),
            DMA((QUAD,)),
            DMA((N,)),
            DMA((N,)),
            DMA((N,)),
            DMA((N,)),
        ],
        compiler_params=pltpu.CompilerParams(
            collective_id=0, has_side_effects=True, vmem_limit_bytes=63 * MIB
        ),
        cost_estimate=pl.CostEstimate(
            flops=2 * R * weights, bytes_accessed=2 * weights, transcendentals=R * VL
        ),
    )(
        slot_of, lengths, hidden, gain.reshape(1, W), queries, new_key, new_value,
        cache_key, cache_value, out_proj, lm_head,
    )
    logits, entropy = pl.pallas_call(
        closing,
        out_shape=(
            jax.ShapeDtypeStruct((R, VL), F32),
            jax.ShapeDtypeStruct((1, R), F32),
        ),
        in_specs=[anywhere, pl.BlockSpec(memory_space=pltpu.VMEM)],
        out_specs=(anywhere, pl.BlockSpec(memory_space=pltpu.VMEM)),
        scratch_shapes=[DMA],
    )(logits, entropy)
    return logits, entropy.reshape(R)


def arrangement(mesh, args):
    NP, NH, NA = mesh.shape["pool"], mesh.shape["head"], mesh.shape["aux"]
    hidden, queries, cache_key, out_proj, lm_head = (
        args[0], args[2], args[5], args[9], args[10],
    )
    R, W = hidden.shape
    S, SPAN = cache_key.shape[:2]
    KV = cache_key.shape[2] // HD
    QL = queries.shape[1] // HD
    VL = lm_head.shape[1]
    HO = out_proj.shape[1] // HD
    fits = (
        R == 8
        and W % 256 == 0
        and VL % out_proj.shape[2] == 0
        and out_proj.shape[1] % W == 0
        and (out_proj.shape[1] // W) % (VL // out_proj.shape[2]) == 0
        and HO % 16 == 0
        and S * HO <= HD
        and QL // KV == 8
        and (KV * S) % 8 == 0
        and SPAN % 128 == 0
        and W * VL * 2 * RING <= 60 * MIB
    )
    if not fits:
        return None
    return dict(
        NP=NP, NH=NH, NA=NA, R=R, S=S, KV=KV, G=QL // KV, SPAN=SPAN, W=W,
        NCH=lm_head.shape[0] // W, NBUF=min(RING, lm_head.shape[0] // W),
    )


def select_rows(onehot, rows):
    return jnp.dot(onehot.astype(jnp.bfloat16), rows, preferred_element_type=jnp.float32).astype(
        jnp.bfloat16
    )


def per_device(
    hidden,
    gain,
    queries,
    new_key,
    new_value,
    cache_key,
    cache_value,
    lengths,
    slot_of,
    out_proj,
    lm_head,
):
    slots_here = cache_key.shape[0]
    span = cache_key.shape[1]
    kv_here = cache_key.shape[2] // HD
    q_here = queries.shape[1] // HD
    group = q_here // kv_here
    heads_out = out_proj.shape[1] // HD
    scale = 1.0 / math.sqrt(HD)
    pool_place = lax.axis_index("pool")
    head_place = lax.axis_index("head")
    all_queries, all_keys, all_values = (
        lax.all_gather(queries, "pool", axis=0, tiled=True),
        lax.all_gather(new_key, "pool", axis=0, tiled=True),
        lax.all_gather(new_value, "pool", axis=0, tiled=True),
    )
    requests = all_queries.shape[0]
    slot_ids = pool_place * slots_here + jnp.arange(slots_here, dtype=jnp.int32)
    chosen = slot_of[None, :] == slot_ids[:, None]
    query_slot = select_rows(chosen, all_queries)
    key_slot = select_rows(chosen, all_keys)
    value_slot = select_rows(chosen, all_values)
    length_slot = jnp.sum(jnp.where(chosen, lengths[None, :], 0), axis=1)
    query_heads = query_slot.reshape(slots_here, kv_here, group, HD)
    keys = cache_key.reshape(slots_here, span, kv_here, HD)
    values = cache_value.reshape(slots_here, span, kv_here, HD)
    scores = (
        jnp.einsum("skgd,stkd->skgt", query_heads, keys, preferred_element_type=jnp.float32) * scale
    )
    position = head_place * span + jnp.arange(span, dtype=jnp.int32)
    live = position[None, :] < length_slot[:, None]
    weights = jnp.where(live[:, None, None, :], jnp.exp(scores), 0.0)
    total = jnp.sum(weights, axis=3).reshape(slots_here, q_here)
    mixed = jnp.einsum(
        "skgt,stkd->skgd", weights.astype(jnp.bfloat16), values, preferred_element_type=jnp.float32
    )
    mixed = mixed.reshape(slots_here, q_here * HD)
    total, mixed = (
        lax.psum(total.astype(jnp.bfloat16), "head").astype(jnp.float32),
        lax.psum(mixed.astype(jnp.bfloat16), "head").astype(jnp.float32),
    )
    total = lax.dynamic_slice_in_dim(total, head_place * heads_out, heads_out, 1)
    mixed = lax.dynamic_slice_in_dim(mixed, head_place * heads_out * HD, heads_out * HD, 1)
    query_own = lax.dynamic_slice_in_dim(query_slot, head_place * heads_out * HD, heads_out * HD, 1)
    query_own = query_own.reshape(slots_here, heads_out, HD).astype(jnp.float32)
    key_spread = jnp.repeat(key_slot.reshape(slots_here, kv_here, HD), group, axis=1)
    value_spread = jnp.repeat(value_slot.reshape(slots_here, kv_here, HD), group, axis=1)
    key_own = lax.dynamic_slice_in_dim(key_spread, head_place * heads_out, heads_out, 1).astype(
        jnp.float32
    )
    value_own = lax.dynamic_slice_in_dim(value_spread, head_place * heads_out, heads_out, 1).astype(
        jnp.float32
    )
    own = jnp.exp(jnp.sum(query_own * key_own, axis=2) * scale)
    total = total + own
    mixed = mixed.reshape(slots_here, heads_out, HD) + own[:, :, None] * value_own
    attended = (mixed / total[:, :, None]).astype(jnp.bfloat16).reshape(slots_here, heads_out * HD)
    outputs = lax.all_gather(attended, "pool", axis=0, tiled=True)
    order = slot_of[:, None] == jnp.arange(requests, dtype=jnp.int32)[None, :]
    by_request = select_rows(order, outputs)
    weight_block = out_proj[0]
    term = jnp.dot(by_request, weight_block, preferred_element_type=jnp.float32)
    projected = lax.psum(term.astype(jnp.bfloat16), ("head", "aux")).astype(jnp.float32)
    block_hidden, block_gain = (
        lax.all_gather(hidden, ("head", "aux"), axis=1, tiled=True),
        lax.all_gather(gain.astype(jnp.bfloat16), ("head", "aux"), axis=0, tiled=True).astype(
            gain.dtype
        ),
    )
    stream = (block_hidden.astype(jnp.float32) + projected).astype(jnp.bfloat16)
    full_stream, full_gain = (
        lax.all_gather(stream, "pool", axis=1, tiled=True),
        lax.all_gather(block_gain.astype(jnp.bfloat16), "pool", axis=0, tiled=True).astype(
            block_gain.dtype
        ),
    )
    stream_wide = full_stream.astype(jnp.float32)
    mean_sq = jnp.mean(stream_wide * stream_wide, axis=1, keepdims=True)
    normed = (stream_wide * lax.rsqrt(mean_sq + 1e-05) * full_gain[None, :]).astype(jnp.bfloat16)
    logits = jnp.dot(normed, lm_head, preferred_element_type=jnp.float32)
    expd = jnp.exp(logits)
    vocab_total, moment = lax.psum(
        (jnp.sum(expd, axis=1), jnp.sum(expd * logits, axis=1)), ("pool", "head", "aux")
    )
    entropy = jnp.log(vocab_total) - moment / vocab_total
    return (logits, entropy)


def solution(mesh):
    in_specs = (
        P("grp", ("pool", "head", "aux")),
        P(("pool", "head", "aux")),
        P(("grp", "pool"), "aux"),
        P(("grp", "pool"), "aux"),
        P(("grp", "pool"), "aux"),
        P(("grp", "pool"), "head", "aux"),
        P(("grp", "pool"), "head", "aux"),
        P("grp"),
        P("grp"),
        P("aux", "head", "pool"),
        P(None, ("pool", "head", "aux")),
    )
    out_specs = (P("grp", ("pool", "head", "aux")), P("grp"))

    def on_device(*args):
        cfg = arrangement(mesh, args)
        if cfg is None:
            return per_device(*args)
        return one_kernel(cfg, *args)

    return jax.shard_map(
        on_device, mesh=mesh, in_specs=in_specs, out_specs=out_specs, check_vma=False
    )
```

```python
import functools
import math

import jax
import jax.numpy as jnp
from jax import lax
from jax.experimental import pallas as pl
from jax.experimental.pallas import tpu as pltpu
from jax.sharding import PartitionSpec as P

HD = 128
MESH = pl.DeviceIdType.MESH
BF = jnp.bfloat16
F32 = jnp.float32
MIB = 1024 * 1024
RING = 15


def iota(shape, axis):
    return lax.broadcasted_iota(jnp.int32, shape, axis)


def mm(a, b):
    return jnp.dot(a, b, preferred_element_type=F32)


def pick(position, scalars):
    out = jnp.full(position.shape, scalars[0], jnp.int32)
    for r in range(1, len(scalars)):
        out = jnp.where(position == r, scalars[r], out)
    return out


def kernel(
    cfg,
    slot_ref,
    len_ref,
    hidden_hbm,
    gain_hbm,
    q_hbm,
    nk_hbm,
    nv_hbm,
    ck_hbm,
    cv_hbm,
    wo_hbm,
    lm_hbm,
    logits_hbm,
    ent_ref,
    ring,
    ck,
    kt,
    cv,
    qv,
    nkv,
    nvv,
    hid,
    gains,
    stage,
    xq,
    send2,
    recv2,
    hidden_quad,
    recv3,
    xs,
    acc,
    xe,
    ring_sem,
    wo_sem,
    in_sem,
    out_sem,
    q_send,
    q_recv,
    g_send,
    g_recv,
    a_send,
    a_recv,
    t_send,
    t_recv,
    h_send,
    h_recv,
    s_send,
    s_recv,
    e_send,
    e_recv,
):
    NP, NH, NA = cfg["NP"], cfg["NH"], cfg["NA"]
    R, S, KV, G, SPAN = cfg["R"], cfg["S"], cfg["KV"], cfg["G"], cfg["SPAN"]
    W, NCH, NBUF = cfg["W"], cfg["NCH"], cfg["NBUF"]
    QL = KV * G
    HO = QL // NH
    QUAD = NH * NA
    scale = 1.0 / math.sqrt(HD)
    p = lax.axis_index("pool")
    h = lax.axis_index("head")
    a = lax.axis_index("aux")
    me = (p * NH + h) * NA + a
    everyone = [
        (dp, dh, da)
        for dp in range(NP)
        for dh in range(NH)
        for da in range(NA)
        if (dp, dh, da) != (0, 0, 0)
    ]

    def at(dp, dh, da):
        return {
            "pool": lax.rem(p + dp, NP),
            "head": lax.rem(h + dh, NH),
            "aux": lax.rem(a + da, NA),
        }

    def place(where):
        return (where["pool"] * NH + where["head"]) * NA + where["aux"]

    barrier = pltpu.get_barrier_semaphore()
    for d in everyone:
        pl.semaphore_signal(barrier, inc=1, device_id=at(*d), device_id_type=MESH)

    ins = [
        pltpu.make_async_copy(src, dst, in_sem.at[i])
        for i, (src, dst) in enumerate(
            [
                (q_hbm, qv),
                (nk_hbm, nkv),
                (nv_hbm, nvv),
                (gain_hbm, gains.at[me]),
                (hidden_hbm, hid),
                (ck_hbm, ck),
                (cv_hbm, cv),
            ]
        )
    ]
    for c in ins:
        c.start()

    DB = wo_hbm.shape[2]
    ROWS, VL = ring.shape[1], ring.shape[2]
    per = VL // DB
    KO = wo_hbm.shape[1]
    pieces = KO // ROWS
    held_slots = pieces // per
    wo_places = [
        (NBUF - held_slots + i // per, (i % per) * DB, i * ROWS) for i in range(pieces)
    ]
    wo_copies = [
        pltpu.make_async_copy(
            wo_hbm.at[0, pl.ds(row, ROWS), :],
            ring.at[slot, :, pl.ds(lane, DB)],
            wo_sem.at[i],
        )
        for i, (slot, lane, row) in enumerate(wo_places)
    ]
    for c in wo_copies:
        c.start()

    def block_of(o):
        return lax.rem(p * QUAD + o, NCH)

    def lm_copy(o, slot):
        row = pl.multiple_of(block_of(o) * ROWS, ROWS)
        return pltpu.make_async_copy(
            lm_hbm.at[pl.ds(row, ROWS), :], ring.at[slot], ring_sem.at[slot]
        )

    free = NBUF - held_slots

    def start_chunks(first, last):
        for o in range(min(first, free), min(last, free)):
            lm_copy(o, o).start(priority=1)

    start_chunks(0, 2)

    for c in ins[:5]:
        c.wait()
    for j in range(QL):
        stage[j * S : (j + 1) * S, :] = qv[:, j * HD : (j + 1) * HD].astype(F32)
    for j in range(KV):
        stage[(QL + j) * S : (QL + j + 1) * S, :] = nkv[:, j * HD : (j + 1) * HD].astype(F32)
        stage[(QL + KV + j) * S : (QL + KV + j + 1) * S, :] = nvv[
            :, j * HD : (j + 1) * HD
        ].astype(F32)
    xq[p] = stage[...].astype(BF)
    mine = h * NA + a
    hidden_quad[mine] = hid[...].astype(F32)

    pl.semaphore_wait(barrier, len(everyone))

    def send(src, dst, ssem, rsem, to):
        c = pltpu.make_async_remote_copy(
            src_ref=src, dst_ref=dst, send_sem=ssem, recv_sem=rsem,
            device_id=to, device_id_type=MESH,
        )
        c.start()
        return c

    sent = []
    q_copies = [
        send(xq.at[p], xq.at[p], q_send.at[d], q_recv.at[d], at(d, 0, 0))
        for d in range(1, NP)
    ]
    sent += q_copies
    for i, d in enumerate(everyone):
        sent.append(send(gains.at[me], gains.at[me], g_send.at[i], g_recv.at[me], at(*d)))
    quad = [d for d in everyone if d[0] == 0]
    h_copies = [
        send(hidden_quad.at[mine], hidden_quad.at[mine], h_send.at[i], h_recv.at[i], at(*d))
        for i, d in enumerate(quad)
    ]
    sent += h_copies
    start_chunks(2, 4)

    slots = [slot_ref[r] for r in range(R)]
    lengths = [len_ref[r] for r in range(R)]
    rows_q = iota((S * QL, NP * QL * S), 0)
    cols_q = iota((S * QL, NP * QL * S), 1)
    req_q = (cols_q // (QL * S)) * S + cols_q % S
    hot_q = jnp.where(
        ((cols_q // S) % QL == rows_q % QL) & (pick(req_q, slots) == p * S + rows_q // QL),
        1.0,
        0.0,
    ).astype(BF)
    M2 = 2 * KV * S
    rows_k = iota((2 * S * QL, NP * M2), 0)
    cols_k = iota((2 * S * QL, NP * M2), 1)
    req_k = (cols_k // M2) * S + cols_k % S
    hot_k = jnp.where(
        ((cols_k // S) % (2 * KV) == (rows_k // (S * QL)) * KV + (rows_k % QL) // G)
        & (pick(req_k, slots) == p * S + (rows_k % (S * QL)) // QL),
        1.0,
        0.0,
    ).astype(BF)
    position = h * SPAN + iota((G, SPAN), 1)
    live = []
    for s in range(S):
        length = jnp.int32(0)
        for r in range(R):
            length = length + jnp.where(slots[r] == p * S + s, lengths[r], 0)
        live.append(position < length)

    ins[5].wait()
    for s in range(S):
        kt[s] = ck[s].T

    for c in q_copies:
        c.wait_recv()
    Xq = xq[:, 0 : QL * S, :].reshape(NP * QL * S, HD)
    Xk = xq[:, QL * S :, :].reshape(NP * M2, HD)
    Qs = mm(hot_q, Xq)
    KVs = mm(hot_k, Xk)
    own = jnp.exp(jnp.sum(Qs * KVs[: S * QL], axis=1, keepdims=True) * scale)
    own = own * jnp.where(h == 0, 1.0, 0.0)

    ins[6].wait()
    total_parts, mixed_parts = [], []
    for s in range(S):
        for k in range(KV):
            at_row = (s * KV + k) * G
            query = Qs[at_row : at_row + G].astype(BF)
            scores = mm(query, kt[s, k * HD : (k + 1) * HD, :])
            weights = jnp.where(live[s], jnp.exp(scores * scale), 0.0)
            total_parts.append(jnp.sum(weights, axis=1, keepdims=True))
            mixed_parts.append(mm(weights.astype(BF), cv[s, :, k * HD : (k + 1) * HD]))
    total = jnp.concatenate(total_parts, axis=0) + own
    mixed = jnp.concatenate(mixed_parts, axis=0) + own * KVs[S * QL :]
    B = S * HO
    diag = iota((B, HD), 0) == iota((B, HD), 1)
    lines = iota((16, HD), 0)
    for t in range(NH):
        column = []
        for s in range(S):
            first = s * QL + t * HO
            send2[t, s * HO : (s + 1) * HO, :] = mixed[first : first + HO].astype(BF)
            column.append(total[first : first + HO])
        column = jnp.concatenate(column, axis=0)
        line = jnp.sum(jnp.where(diag, column, 0.0), axis=0, keepdims=True)
        high = line.astype(BF).astype(F32)
        send2[t, B:, :] = jnp.where(
            lines == 0, high, jnp.where(lines == 1, line - high, 0.0)
        ).astype(BF)
    here = p * NH + h
    recv2[here] = send2[h]
    a_copies = []
    for i, (dp, dh, da) in enumerate([d for d in everyone if d[2] == 0]):
        to = at(dp, dh, 0)
        a_copies.append(
            send(send2.at[to["head"]], recv2.at[here], a_send.at[i], a_recv.at[i], to)
        )
    sent += a_copies
    start_chunks(4, 6)

    RH = iota((HO * R, NP * B), 0)
    CH = iota((HO * R, NP * B), 1)
    order = jnp.where(
        (RH // R == CH % HO) & (pick(RH % R, slots) == CH // HO), 1.0, 0.0
    ).astype(BF)
    for c in a_copies:
        c.wait_recv()
    attended = []
    for q in range(NP):
        got = recv2[q * NH].astype(F32)
        for t in range(1, NH):
            got = got + recv2[q * NH + t].astype(F32)
        line = got[B : B + 1] + got[B + 1 : B + 2]
        column = jnp.sum(jnp.where(diag, line, 0.0), axis=1, keepdims=True)
        attended.append((got[:B] / column).astype(BF))
    by_head = mm(order, jnp.concatenate(attended, axis=0))
    by_request = jnp.concatenate(
        [by_head[j * R : (j + 1) * R] for j in range(HO)], axis=1
    ).astype(BF)

    for c in wo_copies:
        c.wait()
    terms = []
    for n in range(QUAD):
        term = jnp.zeros((R, W), F32)
        for slot, lane, row in wo_places:
            first = lane + n * W
            term = term + mm(by_request[:, row : row + ROWS], ring[slot, :, first : first + W])
        terms.append(term)

    def two_rows(blocks):
        half = len(blocks) // 2
        return jnp.concatenate(
            [jnp.concatenate(blocks[:half], axis=1), jnp.concatenate(blocks[half:], axis=1)],
            axis=0,
        )

    recv3[mine] = two_rows(terms).astype(BF)
    t_copies = [
        send(recv3.at[mine], recv3.at[mine], t_send.at[i], t_recv.at[i], at(*d))
        for i, d in enumerate(quad)
    ]
    sent += t_copies
    start_chunks(6, 8)
    for c in h_copies:
        c.wait_recv()
    stream = two_rows([hidden_quad[n] for n in range(QUAD)])
    for c in t_copies:
        c.wait_recv()
    projected = recv3[0].astype(F32)
    for n in range(1, QUAD):
        projected = projected + recv3[n].astype(F32)
    xs[p] = (stream + projected).astype(BF)
    sent += [
        send(xs.at[p], xs.at[p], s_send.at[d], s_recv.at[p], at(d, 0, 0)) for d in range(1, NP)
    ]
    start_chunks(8, free)
    for o in range(free, NBUF):
        lm_copy(o, o).start(priority=1)

    acc[...] = jnp.zeros_like(acc)

    def arrived(block, sems):
        return pltpu.make_async_remote_copy(
            src_ref=block, dst_ref=block, send_sem=s_send.at[0], recv_sem=sems,
            device_id=at(1, 0, 0), device_id_type=MESH,
        )

    def group(g, squares):
        q = lax.rem(p + g, NP)

        @pl.when(g > 0)
        def _():
            arrived(xs.at[q], s_recv.at[q]).wait_recv()

        for i in range(QUAD):
            b = q * QUAD + i

            @pl.when(b != me)
            def _():
                arrived(gains.at[b], g_recv.at[b]).wait_recv()

        both = xs[q].astype(F32)
        lefts = []
        for i in range(QUAD):
            top = (i // (QUAD // 2)) * R
            lane = (i % (QUAD // 2)) * W
            block = both[top : top + R, lane : lane + W]
            lefts.append((block * gains[q * QUAD + i]).astype(BF))
            squares = squares + jnp.sum(block * block, axis=1, keepdims=True)
        held = [lax.rem(g * QUAD + i, NBUF) for i in range(QUAD)]
        for i in range(QUAD):
            lm_copy(g * QUAD + i, held[i]).wait()
        part = VL // 4
        for first in range(0, VL, part):
            add = mm(lefts[0], ring[held[0], :, first : first + part])
            for i in range(1, QUAD):
                add = add + mm(lefts[i], ring[held[i], :, first : first + part])
            acc[:, first : first + part] += add
        for i in range(QUAD):
            o = g * QUAD + i

            @pl.when(o + NBUF < NCH)
            def _():
                lm_copy(o + NBUF, held[i]).start(priority=1)

        return squares

    squares = lax.fori_loop(0, NCH // QUAD, group, jnp.zeros((R, 1), F32))
    logits = acc[...] * lax.rsqrt(squares * (1.0 / (NCH * ROWS)) + 1e-05)
    acc[...] = logits
    out = pltpu.make_async_copy(acc, logits_hbm, out_sem)
    out.start()
    expd = jnp.exp(logits)
    sums = jnp.sum(expd, axis=1, keepdims=True)
    moments = jnp.sum(expd * logits, axis=1, keepdims=True)
    lane = iota((R, HD), 1)
    xe[me] = jnp.where(lane == 0, sums, jnp.where(lane == 1, moments, 0.0))
    e_copies = [
        send(xe.at[me], xe.at[me], e_send.at[i], e_recv.at[i], at(*d))
        for i, d in enumerate(everyone)
    ]
    sent += e_copies
    for c in e_copies:
        c.wait_recv()
    both = jnp.sum(xe[...], axis=0)
    vocab_total, moment = both[:, 0:1], both[:, 1:2]
    entropy = jnp.log(vocab_total) - moment / vocab_total
    spread = jnp.sum(jnp.where(iota((R, HD), 0) == lane, entropy, 0.0), axis=0, keepdims=True)
    ent_ref[...] = spread[:, :R]
    out.wait()
    for c in sent:
        c.wait_send()


def closing(logits_in, ent_in, logits_out, ent_out):
    logits_out[...] = logits_in[...]
    ent_out[...] = ent_in[...]


def one_kernel(
    cfg,
    hidden, gain, queries, new_key, new_value, cache_key, cache_value, lengths, slot_of,
    out_proj, lm_head,
):
    NP, NH, NA = cfg["NP"], cfg["NH"], cfg["NA"]
    R, S, KV, G, SPAN = cfg["R"], cfg["S"], cfg["KV"], cfg["G"], cfg["SPAN"]
    W, NCH, NBUF = cfg["W"], cfg["NCH"], cfg["NBUF"]
    QL = KV * G
    N = NP * NH * NA
    QUAD = NH * NA
    VL = lm_head.shape[1]
    rows = (QL + 2 * KV) * S
    message = S * (QL // NH) + 16
    DMA = pltpu.SemaphoreType.DMA
    smem = pl.BlockSpec(memory_space=pltpu.SMEM)
    anywhere = pl.BlockSpec(memory_space=pl.ANY)
    weights = lm_head.size + out_proj.size + 2 * cache_key.size
    logits, entropy = pl.pallas_call(
        functools.partial(kernel, cfg),
        out_shape=(
            jax.ShapeDtypeStruct((R, VL), F32),
            jax.ShapeDtypeStruct((1, R), F32),
        ),
        in_specs=[smem, smem] + [anywhere] * 9,
        out_specs=(anywhere, pl.BlockSpec(memory_space=pltpu.VMEM)),
        scratch_shapes=[
            pltpu.VMEM((NBUF, W, VL), BF),
            pltpu.VMEM(cache_key.shape, BF),
            pltpu.VMEM((S, cache_key.shape[2], SPAN), BF),
            pltpu.VMEM(cache_value.shape, BF),
            pltpu.VMEM(queries.shape, BF),
            pltpu.VMEM(new_key.shape, BF),
            pltpu.VMEM(new_value.shape, BF),
            pltpu.VMEM(hidden.shape, BF),
            pltpu.VMEM((N, 1, W), F32),
            pltpu.VMEM((rows, HD), F32),
            pltpu.VMEM((NP, rows, HD), BF),
            pltpu.VMEM((NH, message, HD), BF),
            pltpu.VMEM((NP * NH, message, HD), BF),
            pltpu.VMEM((QUAD, R, W), F32),
            pltpu.VMEM((QUAD, 2 * R, QUAD * W // 2), BF),
            pltpu.VMEM((NP, 2 * R, QUAD * W // 2), BF),
            pltpu.VMEM((R, VL), F32),
            pltpu.VMEM((N, R, HD), F32),
            DMA((NBUF,)),
            DMA((out_proj.shape[1] // W,)),
            DMA((7,)),
            DMA,
            DMA((NP,)),
            DMA((NP,)),
            DMA((N,)),
            DMA((N,)),
            DMA((NP * NH,)),
            DMA((NP * NH,)),
            DMA((QUAD,)),
            DMA((QUAD,)),
            DMA((QUAD,)),
            DMA((QUAD,)),
            DMA((NP,)),
            DMA((NP,)),
            DMA((N,)),
            DMA((N,)),
        ],
        compiler_params=pltpu.CompilerParams(
            collective_id=0, has_side_effects=True, vmem_limit_bytes=63 * MIB
        ),
        cost_estimate=pl.CostEstimate(
            flops=2 * R * weights, bytes_accessed=2 * weights, transcendentals=R * VL
        ),
    )(
        slot_of, lengths, hidden, gain.reshape(1, W), queries, new_key, new_value,
        cache_key, cache_value, out_proj, lm_head,
    )
    logits, entropy = pl.pallas_call(
        closing,
        out_shape=(
            jax.ShapeDtypeStruct((R, VL), F32),
            jax.ShapeDtypeStruct((1, R), F32),
        ),
    )(logits, entropy)
    return logits, entropy.reshape(R)


def arrangement(mesh, args):
    NP, NH, NA = mesh.shape["pool"], mesh.shape["head"], mesh.shape["aux"]
    hidden, queries, cache_key, out_proj, lm_head = (
        args[0], args[2], args[5], args[9], args[10],
    )
    R, W = hidden.shape
    S, SPAN = cache_key.shape[:2]
    KV = cache_key.shape[2] // HD
    QL = queries.shape[1] // HD
    VL = lm_head.shape[1]
    HO = out_proj.shape[1] // HD
    fits = (
        R == 8
        and W % 256 == 0
        and VL % out_proj.shape[2] == 0
        and out_proj.shape[1] % W == 0
        and (out_proj.shape[1] // W) % (VL // out_proj.shape[2]) == 0
        and HO % 16 == 0
        and S * HO <= HD
        and QL // KV == 8
        and (KV * S) % 8 == 0
        and SPAN % 128 == 0
        and NH * NA % 2 == 0
        and NP * NH * NA * W == lm_head.shape[0]
        and out_proj.shape[2] == NH * NA * W
        and W * VL * 2 * RING <= 60 * MIB
    )
    if not fits:
        return None
    return dict(
        NP=NP, NH=NH, NA=NA, R=R, S=S, KV=KV, G=QL // KV, SPAN=SPAN, W=W,
        NCH=lm_head.shape[0] // W, NBUF=min(RING, lm_head.shape[0] // W),
    )


def select_rows(onehot, rows):
    return jnp.dot(onehot.astype(jnp.bfloat16), rows, preferred_element_type=jnp.float32).astype(
        jnp.bfloat16
    )


def per_device(
    hidden,
    gain,
    queries,
    new_key,
    new_value,
    cache_key,
    cache_value,
    lengths,
    slot_of,
    out_proj,
    lm_head,
):
    slots_here = cache_key.shape[0]
    span = cache_key.shape[1]
    kv_here = cache_key.shape[2] // HD
    q_here = queries.shape[1] // HD
    group = q_here // kv_here
    heads_out = out_proj.shape[1] // HD
    scale = 1.0 / math.sqrt(HD)
    pool_place = lax.axis_index("pool")
    head_place = lax.axis_index("head")
    all_queries, all_keys, all_values = (
        lax.all_gather(queries, "pool", axis=0, tiled=True),
        lax.all_gather(new_key, "pool", axis=0, tiled=True),
        lax.all_gather(new_value, "pool", axis=0, tiled=True),
    )
    requests = all_queries.shape[0]
    slot_ids = pool_place * slots_here + jnp.arange(slots_here, dtype=jnp.int32)
    chosen = slot_of[None, :] == slot_ids[:, None]
    query_slot = select_rows(chosen, all_queries)
    key_slot = select_rows(chosen, all_keys)
    value_slot = select_rows(chosen, all_values)
    length_slot = jnp.sum(jnp.where(chosen, lengths[None, :], 0), axis=1)
    query_heads = query_slot.reshape(slots_here, kv_here, group, HD)
    keys = cache_key.reshape(slots_here, span, kv_here, HD)
    values = cache_value.reshape(slots_here, span, kv_here, HD)
    scores = (
        jnp.einsum("skgd,stkd->skgt", query_heads, keys, preferred_element_type=jnp.float32) * scale
    )
    position = head_place * span + jnp.arange(span, dtype=jnp.int32)
    live = position[None, :] < length_slot[:, None]
    weights = jnp.where(live[:, None, None, :], jnp.exp(scores), 0.0)
    total = jnp.sum(weights, axis=3).reshape(slots_here, q_here)
    mixed = jnp.einsum(
        "skgt,stkd->skgd", weights.astype(jnp.bfloat16), values, preferred_element_type=jnp.float32
    )
    mixed = mixed.reshape(slots_here, q_here * HD)
    total, mixed = (
        lax.psum(total.astype(jnp.bfloat16), "head").astype(jnp.float32),
        lax.psum(mixed.astype(jnp.bfloat16), "head").astype(jnp.float32),
    )
    total = lax.dynamic_slice_in_dim(total, head_place * heads_out, heads_out, 1)
    mixed = lax.dynamic_slice_in_dim(mixed, head_place * heads_out * HD, heads_out * HD, 1)
    query_own = lax.dynamic_slice_in_dim(query_slot, head_place * heads_out * HD, heads_out * HD, 1)
    query_own = query_own.reshape(slots_here, heads_out, HD).astype(jnp.float32)
    key_spread = jnp.repeat(key_slot.reshape(slots_here, kv_here, HD), group, axis=1)
    value_spread = jnp.repeat(value_slot.reshape(slots_here, kv_here, HD), group, axis=1)
    key_own = lax.dynamic_slice_in_dim(key_spread, head_place * heads_out, heads_out, 1).astype(
        jnp.float32
    )
    value_own = lax.dynamic_slice_in_dim(value_spread, head_place * heads_out, heads_out, 1).astype(
        jnp.float32
    )
    own = jnp.exp(jnp.sum(query_own * key_own, axis=2) * scale)
    total = total + own
    mixed = mixed.reshape(slots_here, heads_out, HD) + own[:, :, None] * value_own
    attended = (mixed / total[:, :, None]).astype(jnp.bfloat16).reshape(slots_here, heads_out * HD)
    outputs = lax.all_gather(attended, "pool", axis=0, tiled=True)
    order = slot_of[:, None] == jnp.arange(requests, dtype=jnp.int32)[None, :]
    by_request = select_rows(order, outputs)
    weight_block = out_proj[0]
    term = jnp.dot(by_request, weight_block, preferred_element_type=jnp.float32)
    projected = lax.psum(term.astype(jnp.bfloat16), ("head", "aux")).astype(jnp.float32)
    block_hidden, block_gain = (
        lax.all_gather(hidden, ("head", "aux"), axis=1, tiled=True),
        lax.all_gather(gain.astype(jnp.bfloat16), ("head", "aux"), axis=0, tiled=True).astype(
            gain.dtype
        ),
    )
    stream = (block_hidden.astype(jnp.float32) + projected).astype(jnp.bfloat16)
    full_stream, full_gain = (
        lax.all_gather(stream, "pool", axis=1, tiled=True),
        lax.all_gather(block_gain.astype(jnp.bfloat16), "pool", axis=0, tiled=True).astype(
            block_gain.dtype
        ),
    )
    stream_wide = full_stream.astype(jnp.float32)
    mean_sq = jnp.mean(stream_wide * stream_wide, axis=1, keepdims=True)
    normed = (stream_wide * lax.rsqrt(mean_sq + 1e-05) * full_gain[None, :]).astype(jnp.bfloat16)
    logits = jnp.dot(normed, lm_head, preferred_element_type=jnp.float32)
    expd = jnp.exp(logits)
    vocab_total, moment = lax.psum(
        (jnp.sum(expd, axis=1), jnp.sum(expd * logits, axis=1)), ("pool", "head", "aux")
    )
    entropy = jnp.log(vocab_total) - moment / vocab_total
    return (logits, entropy)


def solution(mesh):
    in_specs = (
        P("grp", ("pool", "head", "aux")),
        P(("pool", "head", "aux")),
        P(("grp", "pool"), "aux"),
        P(("grp", "pool"), "aux"),
        P(("grp", "pool"), "aux"),
        P(("grp", "pool"), "head", "aux"),
        P(("grp", "pool"), "head", "aux"),
        P("grp"),
        P("grp"),
        P("aux", "head", "pool"),
        P(None, ("pool", "head", "aux")),
    )
    out_specs = (P("grp", ("pool", "head", "aux")), P("grp"))

    def on_device(*args):
        cfg = arrangement(mesh, args)
        if cfg is None:
            return per_device(*args)
        return one_kernel(cfg, *args)

    return jax.shard_map(
        on_device, mesh=mesh, in_specs=in_specs, out_specs=out_specs, check_vma=False
    )
```

```python
import functools
import math

import jax
import jax.numpy as jnp
from jax import lax
from jax.experimental import pallas as pl
from jax.experimental.pallas import tpu as pltpu
from jax.sharding import PartitionSpec as P

HD = 128
MESH = pl.DeviceIdType.MESH
BF = jnp.bfloat16
F32 = jnp.float32
MIB = 1024 * 1024
RING = 15


def iota(shape, axis):
    return lax.broadcasted_iota(jnp.int32, shape, axis)


def mm(a, b):
    return jnp.dot(a, b, preferred_element_type=F32)


def pick(position, scalars):
    out = jnp.full(position.shape, scalars[0], jnp.int32)
    for r in range(1, len(scalars)):
        out = jnp.where(position == r, scalars[r], out)
    return out


def kernel(
    cfg,
    slot_ref,
    len_ref,
    hidden_hbm,
    gain_hbm,
    q_hbm,
    nk_hbm,
    nv_hbm,
    ck_hbm,
    cv_hbm,
    wo_hbm,
    lm_hbm,
    logits_hbm,
    ent_ref,
    ring,
    ck,
    kt,
    cv,
    qv,
    nkv,
    nvv,
    hid,
    gains,
    stage,
    xq,
    send2,
    recv2,
    hidden_quad,
    recv3,
    xs,
    acc,
    xe,
    ring_sem,
    wo_sem,
    in_sem,
    out_sem,
    q_send,
    q_recv,
    g_send,
    g_recv,
    a_send,
    a_recv,
    t_send,
    t_recv,
    h_send,
    h_recv,
    s_send,
    s_recv,
    e_send,
    e_recv,
):
    NP, NH, NA = cfg["NP"], cfg["NH"], cfg["NA"]
    R, S, KV, G, SPAN = cfg["R"], cfg["S"], cfg["KV"], cfg["G"], cfg["SPAN"]
    W, NCH, NBUF = cfg["W"], cfg["NCH"], cfg["NBUF"]
    QL = KV * G
    HO = QL // NH
    QUAD = NH * NA
    scale = 1.0 / math.sqrt(HD)
    p = lax.axis_index("pool")
    h = lax.axis_index("head")
    a = lax.axis_index("aux")
    me = (p * NH + h) * NA + a
    everyone = [
        (dp, dh, da)
        for dp in range(NP)
        for dh in range(NH)
        for da in range(NA)
        if (dp, dh, da) != (0, 0, 0)
    ]

    def at(dp, dh, da):
        return {
            "pool": lax.rem(p + dp, NP),
            "head": lax.rem(h + dh, NH),
            "aux": lax.rem(a + da, NA),
        }

    def place(where):
        return (where["pool"] * NH + where["head"]) * NA + where["aux"]

    barrier = pltpu.get_barrier_semaphore()
    for d in everyone:
        pl.semaphore_signal(barrier, inc=1, device_id=at(*d), device_id_type=MESH)

    ins = [
        pltpu.make_async_copy(src, dst, in_sem.at[i])
        for i, (src, dst) in enumerate(
            [
                (q_hbm, qv),
                (nk_hbm, nkv),
                (nv_hbm, nvv),
                (gain_hbm, gains.at[me]),
                (hidden_hbm, hid),
                (ck_hbm, ck),
                (cv_hbm, cv),
            ]
        )
    ]
    for c in ins:
        c.start()

    DB = wo_hbm.shape[2]
    ROWS, VL = ring.shape[1], ring.shape[2]
    per = VL // DB
    KO = wo_hbm.shape[1]
    pieces = KO // ROWS
    held_slots = pieces // per
    wo_places = [
        (NBUF - held_slots + i // per, (i % per) * DB, i * ROWS) for i in range(pieces)
    ]
    wo_copies = [
        pltpu.make_async_copy(
            wo_hbm.at[0, pl.ds(row, ROWS), :],
            ring.at[slot, :, pl.ds(lane, DB)],
            wo_sem.at[i],
        )
        for i, (slot, lane, row) in enumerate(wo_places)
    ]
    for c in wo_copies:
        c.start()

    def block_of(o):
        return lax.rem(p * QUAD + o, NCH)

    def lm_copy(o, slot):
        row = pl.multiple_of(block_of(o) * ROWS, ROWS)
        return pltpu.make_async_copy(
            lm_hbm.at[pl.ds(row, ROWS), :], ring.at[slot], ring_sem.at[slot]
        )

    free = NBUF - held_slots

    def start_chunks(first, last):
        for o in range(min(first, free), min(last, free)):
            lm_copy(o, o).start(priority=1)

    start_chunks(0, 2)

    for c in ins[:5]:
        c.wait()
    for j in range(QL):
        stage[j * S : (j + 1) * S, :] = qv[:, j * HD : (j + 1) * HD].astype(F32)
    for j in range(KV):
        stage[(QL + j) * S : (QL + j + 1) * S, :] = nkv[:, j * HD : (j + 1) * HD].astype(F32)
        stage[(QL + KV + j) * S : (QL + KV + j + 1) * S, :] = nvv[
            :, j * HD : (j + 1) * HD
        ].astype(F32)
    xq[p] = stage[...].astype(BF)
    mine = h * NA + a
    hidden_quad[mine] = hid[...].astype(F32)

    pl.semaphore_wait(barrier, len(everyone))

    def send(src, dst, ssem, rsem, to):
        c = pltpu.make_async_remote_copy(
            src_ref=src, dst_ref=dst, send_sem=ssem, recv_sem=rsem,
            device_id=to, device_id_type=MESH,
        )
        c.start()
        return c

    sent = []
    q_copies = [
        send(xq.at[p], xq.at[p], q_send.at[d], q_recv.at[d], at(d, 0, 0))
        for d in range(1, NP)
    ]
    sent += q_copies
    for i, d in enumerate(everyone):
        sent.append(send(gains.at[me], gains.at[me], g_send.at[i], g_recv.at[me], at(*d)))
    quad = [d for d in everyone if d[0] == 0]
    h_copies = [
        send(hidden_quad.at[mine], hidden_quad.at[mine], h_send.at[i], h_recv.at[i], at(*d))
        for i, d in enumerate(quad)
    ]
    sent += h_copies
    start_chunks(2, 5)

    slots = [slot_ref[r] for r in range(R)]
    lengths = [len_ref[r] for r in range(R)]
    rows_q = iota((S * QL, NP * QL * S), 0)
    cols_q = iota((S * QL, NP * QL * S), 1)
    req_q = (cols_q // (QL * S)) * S + cols_q % S
    hot_q = jnp.where(
        ((cols_q // S) % QL == rows_q % QL) & (pick(req_q, slots) == p * S + rows_q // QL),
        1.0,
        0.0,
    ).astype(BF)
    M2 = 2 * KV * S
    rows_k = iota((2 * S * QL, NP * M2), 0)
    cols_k = iota((2 * S * QL, NP * M2), 1)
    req_k = (cols_k // M2) * S + cols_k % S
    hot_k = jnp.where(
        ((cols_k // S) % (2 * KV) == (rows_k // (S * QL)) * KV + (rows_k % QL) // G)
        & (pick(req_k, slots) == p * S + (rows_k % (S * QL)) // QL),
        1.0,
        0.0,
    ).astype(BF)
    position = h * SPAN + iota((G, SPAN), 1)
    live = []
    for s in range(S):
        length = jnp.int32(0)
        for r in range(R):
            length = length + jnp.where(slots[r] == p * S + s, lengths[r], 0)
        live.append(position < length)

    ins[5].wait()
    for s in range(S):
        kt[s] = ck[s].T

    for c in q_copies:
        c.wait_recv()
    Xq = xq[:, 0 : QL * S, :].reshape(NP * QL * S, HD)
    Xk = xq[:, QL * S :, :].reshape(NP * M2, HD)
    Qs = mm(hot_q, Xq)
    KVs = mm(hot_k, Xk)
    own = jnp.exp(jnp.sum(Qs * KVs[: S * QL], axis=1, keepdims=True) * scale)
    own = own * jnp.where(h == 0, 1.0, 0.0)

    ins[6].wait()
    total_parts, mixed_parts = [], []
    for s in range(S):
        for k in range(KV):
            at_row = (s * KV + k) * G
            query = Qs[at_row : at_row + G].astype(BF)
            scores = mm(query, kt[s, k * HD : (k + 1) * HD, :])
            weights = jnp.where(live[s], jnp.exp(scores * scale), 0.0)
            total_parts.append(jnp.sum(weights, axis=1, keepdims=True))
            mixed_parts.append(mm(weights.astype(BF), cv[s, :, k * HD : (k + 1) * HD]))
    total = jnp.concatenate(total_parts, axis=0) + own
    mixed = jnp.concatenate(mixed_parts, axis=0) + own * KVs[S * QL :]
    B = S * HO
    diag = iota((B, HD), 0) == iota((B, HD), 1)
    lines = iota((16, HD), 0)
    for t in range(NH):
        column = []
        for s in range(S):
            first = s * QL + t * HO
            send2[t, s * HO : (s + 1) * HO, :] = mixed[first : first + HO].astype(BF)
            column.append(total[first : first + HO])
        column = jnp.concatenate(column, axis=0)
        line = jnp.sum(jnp.where(diag, column, 0.0), axis=0, keepdims=True)
        high = line.astype(BF).astype(F32)
        send2[t, B:, :] = jnp.where(
            lines == 0, high, jnp.where(lines == 1, line - high, 0.0)
        ).astype(BF)
    here = p * NH + h
    recv2[here] = send2[h]
    a_copies = []
    for i, (dp, dh, da) in enumerate([d for d in everyone if d[2] == 0]):
        to = at(dp, dh, 0)
        a_copies.append(
            send(send2.at[to["head"]], recv2.at[here], a_send.at[i], a_recv.at[i], to)
        )
    sent += a_copies
    start_chunks(5, 9)

    RH = iota((HO * R, NP * B), 0)
    CH = iota((HO * R, NP * B), 1)
    order = jnp.where(
        (RH // R == CH % HO) & (pick(RH % R, slots) == CH // HO), 1.0, 0.0
    ).astype(BF)
    for c in a_copies:
        c.wait_recv()
    attended = []
    for q in range(NP):
        got = recv2[q * NH].astype(F32)
        for t in range(1, NH):
            got = got + recv2[q * NH + t].astype(F32)
        line = got[B : B + 1] + got[B + 1 : B + 2]
        column = jnp.sum(jnp.where(diag, line, 0.0), axis=1, keepdims=True)
        attended.append((got[:B] / column).astype(BF))
    by_head = mm(order, jnp.concatenate(attended, axis=0))
    by_request = jnp.concatenate(
        [by_head[j * R : (j + 1) * R] for j in range(HO)], axis=1
    ).astype(BF)

    for c in wo_copies:
        c.wait()
    terms = []
    for n in range(QUAD):
        term = jnp.zeros((R, W), F32)
        for slot, lane, row in wo_places:
            first = lane + n * W
            term = term + mm(by_request[:, row : row + ROWS], ring[slot, :, first : first + W])
        terms.append(term)

    def two_rows(blocks):
        half = len(blocks) // 2
        return jnp.concatenate(
            [jnp.concatenate(blocks[:half], axis=1), jnp.concatenate(blocks[half:], axis=1)],
            axis=0,
        )

    recv3[mine] = two_rows(terms).astype(BF)
    t_copies = [
        send(recv3.at[mine], recv3.at[mine], t_send.at[i], t_recv.at[i], at(*d))
        for i, d in enumerate(quad)
    ]
    sent += t_copies
    start_chunks(9, free)
    for c in h_copies:
        c.wait_recv()
    stream = two_rows([hidden_quad[n] for n in range(QUAD)])
    for c in t_copies:
        c.wait_recv()
    projected = recv3[0].astype(F32)
    for n in range(1, QUAD):
        projected = projected + recv3[n].astype(F32)
    xs[p] = (stream + projected).astype(BF)
    sent += [
        send(xs.at[p], xs.at[p], s_send.at[d], s_recv.at[p], at(d, 0, 0)) for d in range(1, NP)
    ]
    for o in range(free, NBUF):
        lm_copy(o, o).start(priority=1)

    acc[...] = jnp.zeros_like(acc)

    def arrived(block, sems):
        return pltpu.make_async_remote_copy(
            src_ref=block, dst_ref=block, send_sem=s_send.at[0], recv_sem=sems,
            device_id=at(1, 0, 0), device_id_type=MESH,
        )

    def group(g, squares):
        q = lax.rem(p + g, NP)

        @pl.when(g > 0)
        def _():
            arrived(xs.at[q], s_recv.at[q]).wait_recv()

        for i in range(QUAD):
            b = q * QUAD + i

            @pl.when(b != me)
            def _():
                arrived(gains.at[b], g_recv.at[b]).wait_recv()

        both = xs[q].astype(F32)
        lefts = []
        for i in range(QUAD):
            top = (i // (QUAD // 2)) * R
            lane = (i % (QUAD // 2)) * W
            block = both[top : top + R, lane : lane + W]
            lefts.append((block * gains[q * QUAD + i]).astype(BF))
            squares = squares + jnp.sum(block * block, axis=1, keepdims=True)
        held = [lax.rem(g * QUAD + i, NBUF) for i in range(QUAD)]
        part = VL // 4
        for pair in range(0, QUAD, 2):
            for i in (pair, pair + 1):
                lm_copy(g * QUAD + i, held[i]).wait()
            for first in range(0, VL, part):
                add = mm(lefts[pair], ring[held[pair], :, first : first + part])
                add = add + mm(lefts[pair + 1], ring[held[pair + 1], :, first : first + part])
                acc[:, first : first + part] += add
            for i in (pair, pair + 1):
                o = g * QUAD + i

                @pl.when(o + NBUF < NCH)
                def _():
                    lm_copy(o + NBUF, held[i]).start(priority=1)

        return squares

    squares = lax.fori_loop(0, NCH // QUAD, group, jnp.zeros((R, 1), F32))
    logits = acc[...] * lax.rsqrt(squares * (1.0 / (NCH * ROWS)) + 1e-05)
    acc[...] = logits
    out = pltpu.make_async_copy(acc, logits_hbm, out_sem)
    out.start()
    expd = jnp.exp(logits)
    sums = jnp.sum(expd, axis=1, keepdims=True)
    moments = jnp.sum(expd * logits, axis=1, keepdims=True)
    lane = iota((R, HD), 1)
    xe[me] = jnp.where(lane == 0, sums, jnp.where(lane == 1, moments, 0.0))
    e_copies = [
        send(xe.at[me], xe.at[me], e_send.at[i], e_recv.at[i], at(*d))
        for i, d in enumerate(everyone)
    ]
    sent += e_copies
    for c in e_copies:
        c.wait_recv()
    both = jnp.sum(xe[...], axis=0)
    vocab_total, moment = both[:, 0:1], both[:, 1:2]
    entropy = jnp.log(vocab_total) - moment / vocab_total
    spread = jnp.sum(jnp.where(iota((R, HD), 0) == lane, entropy, 0.0), axis=0, keepdims=True)
    ent_ref[...] = spread[:, :R]
    out.wait()
    for c in sent:
        c.wait_send()


def closing(logits_in, ent_in, logits_out, ent_out):
    logits_out[...] = logits_in[...]
    ent_out[...] = ent_in[...]


def one_kernel(
    cfg,
    hidden, gain, queries, new_key, new_value, cache_key, cache_value, lengths, slot_of,
    out_proj, lm_head,
):
    NP, NH, NA = cfg["NP"], cfg["NH"], cfg["NA"]
    R, S, KV, G, SPAN = cfg["R"], cfg["S"], cfg["KV"], cfg["G"], cfg["SPAN"]
    W, NCH, NBUF = cfg["W"], cfg["NCH"], cfg["NBUF"]
    QL = KV * G
    N = NP * NH * NA
    QUAD = NH * NA
    VL = lm_head.shape[1]
    rows = (QL + 2 * KV) * S
    message = S * (QL // NH) + 16
    DMA = pltpu.SemaphoreType.DMA
    smem = pl.BlockSpec(memory_space=pltpu.SMEM)
    anywhere = pl.BlockSpec(memory_space=pl.ANY)
    weights = lm_head.size + out_proj.size + 2 * cache_key.size
    logits, entropy = pl.pallas_call(
        functools.partial(kernel, cfg),
        out_shape=(
            jax.ShapeDtypeStruct((R, VL), F32),
            jax.ShapeDtypeStruct((1, R), F32),
        ),
        in_specs=[smem, smem] + [anywhere] * 9,
        out_specs=(anywhere, pl.BlockSpec(memory_space=pltpu.VMEM)),
        scratch_shapes=[
            pltpu.VMEM((NBUF, W, VL), BF),
            pltpu.VMEM(cache_key.shape, BF),
            pltpu.VMEM((S, cache_key.shape[2], SPAN), BF),
            pltpu.VMEM(cache_value.shape, BF),
            pltpu.VMEM(queries.shape, BF),
            pltpu.VMEM(new_key.shape, BF),
            pltpu.VMEM(new_value.shape, BF),
            pltpu.VMEM(hidden.shape, BF),
            pltpu.VMEM((N, 1, W), F32),
            pltpu.VMEM((rows, HD), F32),
            pltpu.VMEM((NP, rows, HD), BF),
            pltpu.VMEM((NH, message, HD), BF),
            pltpu.VMEM((NP * NH, message, HD), BF),
            pltpu.VMEM((QUAD, R, W), F32),
            pltpu.VMEM((QUAD, 2 * R, QUAD * W // 2), BF),
            pltpu.VMEM((NP, 2 * R, QUAD * W // 2), BF),
            pltpu.VMEM((R, VL), F32),
            pltpu.VMEM((N, R, HD), F32),
            DMA((NBUF,)),
            DMA((out_proj.shape[1] // W,)),
            DMA((7,)),
            DMA,
            DMA((NP,)),
            DMA((NP,)),
            DMA((N,)),
            DMA((N,)),
            DMA((NP * NH,)),
            DMA((NP * NH,)),
            DMA((QUAD,)),
            DMA((QUAD,)),
            DMA((QUAD,)),
            DMA((QUAD,)),
            DMA((NP,)),
            DMA((NP,)),
            DMA((N,)),
            DMA((N,)),
        ],
        compiler_params=pltpu.CompilerParams(
            collective_id=0, has_side_effects=True, vmem_limit_bytes=63 * MIB
        ),
        cost_estimate=pl.CostEstimate(
            flops=2 * R * weights, bytes_accessed=2 * weights, transcendentals=R * VL
        ),
    )(
        slot_of, lengths, hidden, gain.reshape(1, W), queries, new_key, new_value,
        cache_key, cache_value, out_proj, lm_head,
    )
    logits, entropy = pl.pallas_call(
        closing,
        out_shape=(
            jax.ShapeDtypeStruct((R, VL), F32),
            jax.ShapeDtypeStruct((1, R), F32),
        ),
    )(logits, entropy)
    return logits, entropy.reshape(R)


def arrangement(mesh, args):
    NP, NH, NA = mesh.shape["pool"], mesh.shape["head"], mesh.shape["aux"]
    hidden, queries, cache_key, out_proj, lm_head = (
        args[0], args[2], args[5], args[9], args[10],
    )
    R, W = hidden.shape
    S, SPAN = cache_key.shape[:2]
    KV = cache_key.shape[2] // HD
    QL = queries.shape[1] // HD
    VL = lm_head.shape[1]
    HO = out_proj.shape[1] // HD
    fits = (
        R == 8
        and W % 256 == 0
        and VL % out_proj.shape[2] == 0
        and out_proj.shape[1] % W == 0
        and (out_proj.shape[1] // W) % (VL // out_proj.shape[2]) == 0
        and HO % 16 == 0
        and S * HO <= HD
        and QL // KV == 8
        and (KV * S) % 8 == 0
        and SPAN % 128 == 0
        and NH * NA % 2 == 0
        and NP * NH * NA * W == lm_head.shape[0]
        and out_proj.shape[2] == NH * NA * W
        and W * VL * 2 * RING <= 60 * MIB
    )
    if not fits:
        return None
    return dict(
        NP=NP, NH=NH, NA=NA, R=R, S=S, KV=KV, G=QL // KV, SPAN=SPAN, W=W,
        NCH=lm_head.shape[0] // W, NBUF=min(RING, lm_head.shape[0] // W),
    )


def select_rows(onehot, rows):
    return jnp.dot(onehot.astype(jnp.bfloat16), rows, preferred_element_type=jnp.float32).astype(
        jnp.bfloat16
    )


def per_device(
    hidden,
    gain,
    queries,
    new_key,
    new_value,
    cache_key,
    cache_value,
    lengths,
    slot_of,
    out_proj,
    lm_head,
):
    slots_here = cache_key.shape[0]
    span = cache_key.shape[1]
    kv_here = cache_key.shape[2] // HD
    q_here = queries.shape[1] // HD
    group = q_here // kv_here
    heads_out = out_proj.shape[1] // HD
    scale = 1.0 / math.sqrt(HD)
    pool_place = lax.axis_index("pool")
    head_place = lax.axis_index("head")
    all_queries, all_keys, all_values = (
        lax.all_gather(queries, "pool", axis=0, tiled=True),
        lax.all_gather(new_key, "pool", axis=0, tiled=True),
        lax.all_gather(new_value, "pool", axis=0, tiled=True),
    )
    requests = all_queries.shape[0]
    slot_ids = pool_place * slots_here + jnp.arange(slots_here, dtype=jnp.int32)
    chosen = slot_of[None, :] == slot_ids[:, None]
    query_slot = select_rows(chosen, all_queries)
    key_slot = select_rows(chosen, all_keys)
    value_slot = select_rows(chosen, all_values)
    length_slot = jnp.sum(jnp.where(chosen, lengths[None, :], 0), axis=1)
    query_heads = query_slot.reshape(slots_here, kv_here, group, HD)
    keys = cache_key.reshape(slots_here, span, kv_here, HD)
    values = cache_value.reshape(slots_here, span, kv_here, HD)
    scores = (
        jnp.einsum("skgd,stkd->skgt", query_heads, keys, preferred_element_type=jnp.float32) * scale
    )
    position = head_place * span + jnp.arange(span, dtype=jnp.int32)
    live = position[None, :] < length_slot[:, None]
    weights = jnp.where(live[:, None, None, :], jnp.exp(scores), 0.0)
    total = jnp.sum(weights, axis=3).reshape(slots_here, q_here)
    mixed = jnp.einsum(
        "skgt,stkd->skgd", weights.astype(jnp.bfloat16), values, preferred_element_type=jnp.float32
    )
    mixed = mixed.reshape(slots_here, q_here * HD)
    total, mixed = (
        lax.psum(total.astype(jnp.bfloat16), "head").astype(jnp.float32),
        lax.psum(mixed.astype(jnp.bfloat16), "head").astype(jnp.float32),
    )
    total = lax.dynamic_slice_in_dim(total, head_place * heads_out, heads_out, 1)
    mixed = lax.dynamic_slice_in_dim(mixed, head_place * heads_out * HD, heads_out * HD, 1)
    query_own = lax.dynamic_slice_in_dim(query_slot, head_place * heads_out * HD, heads_out * HD, 1)
    query_own = query_own.reshape(slots_here, heads_out, HD).astype(jnp.float32)
    key_spread = jnp.repeat(key_slot.reshape(slots_here, kv_here, HD), group, axis=1)
    value_spread = jnp.repeat(value_slot.reshape(slots_here, kv_here, HD), group, axis=1)
    key_own = lax.dynamic_slice_in_dim(key_spread, head_place * heads_out, heads_out, 1).astype(
        jnp.float32
    )
    value_own = lax.dynamic_slice_in_dim(value_spread, head_place * heads_out, heads_out, 1).astype(
        jnp.float32
    )
    own = jnp.exp(jnp.sum(query_own * key_own, axis=2) * scale)
    total = total + own
    mixed = mixed.reshape(slots_here, heads_out, HD) + own[:, :, None] * value_own
    attended = (mixed / total[:, :, None]).astype(jnp.bfloat16).reshape(slots_here, heads_out * HD)
    outputs = lax.all_gather(attended, "pool", axis=0, tiled=True)
    order = slot_of[:, None] == jnp.arange(requests, dtype=jnp.int32)[None, :]
    by_request = select_rows(order, outputs)
    weight_block = out_proj[0]
    term = jnp.dot(by_request, weight_block, preferred_element_type=jnp.float32)
    projected = lax.psum(term.astype(jnp.bfloat16), ("head", "aux")).astype(jnp.float32)
    block_hidden, block_gain = (
        lax.all_gather(hidden, ("head", "aux"), axis=1, tiled=True),
        lax.all_gather(gain.astype(jnp.bfloat16), ("head", "aux"), axis=0, tiled=True).astype(
            gain.dtype
        ),
    )
    stream = (block_hidden.astype(jnp.float32) + projected).astype(jnp.bfloat16)
    full_stream, full_gain = (
        lax.all_gather(stream, "pool", axis=1, tiled=True),
        lax.all_gather(block_gain.astype(jnp.bfloat16), "pool", axis=0, tiled=True).astype(
            block_gain.dtype
        ),
    )
    stream_wide = full_stream.astype(jnp.float32)
    mean_sq = jnp.mean(stream_wide * stream_wide, axis=1, keepdims=True)
    normed = (stream_wide * lax.rsqrt(mean_sq + 1e-05) * full_gain[None, :]).astype(jnp.bfloat16)
    logits = jnp.dot(normed, lm_head, preferred_element_type=jnp.float32)
    expd = jnp.exp(logits)
    vocab_total, moment = lax.psum(
        (jnp.sum(expd, axis=1), jnp.sum(expd * logits, axis=1)), ("pool", "head", "aux")
    )
    entropy = jnp.log(vocab_total) - moment / vocab_total
    return (logits, entropy)


def solution(mesh):
    in_specs = (
        P("grp", ("pool", "head", "aux")),
        P(("pool", "head", "aux")),
        P(("grp", "pool"), "aux"),
        P(("grp", "pool"), "aux"),
        P(("grp", "pool"), "aux"),
        P(("grp", "pool"), "head", "aux"),
        P(("grp", "pool"), "head", "aux"),
        P("grp"),
        P("grp"),
        P("aux", "head", "pool"),
        P(None, ("pool", "head", "aux")),
    )
    out_specs = (P("grp", ("pool", "head", "aux")), P("grp"))

    def on_device(*args):
        cfg = arrangement(mesh, args)
        if cfg is None:
            return per_device(*args)
        return one_kernel(cfg, *args)

    return jax.shard_map(
        on_device, mesh=mesh, in_specs=in_specs, out_specs=out_specs, check_vma=False
    )
```
